512 devices in a mesh: seq: 512 (over x, z, y, core).
Axes of the slice: x: 4, y: 4, z: 16, core: 2. Of those that a mesh axis runs over, the one named last changes fastest.
Arguments:
- hidden: bfloat16 [65536, 2048], P('seq'), may hold values from -24 to 24
- queries: bfloat16 [65536, 2048], P('seq'), may hold values from -6 to 6
- key_rows: bfloat16 [65536, 512], P('seq'), may hold values from -6 to 6
- grad_out: bfloat16 [65536, 2048], P('seq'), may hold values from -6 to 6
- master_value: float32 [2048, 512], P('seq'), may hold values from -0.125 to 0.125
- adam_first: float32 [2048, 512], P('seq'), may hold values from -12 to 12
- adam_second: float32 [2048, 512], P('seq'), may hold values from 1 to 100
Outputs:
- attention: bfloat16 [65536, 2048], P('seq')
- grad_queries: bfloat16 [65536, 2048], P('seq')
- grad_keys: bfloat16 [65536, 512], P('seq')
- grad_hidden: bfloat16 [65536, 2048], P('seq')
- new_master: float32 [2048, 512], P('seq')
- new_first: float32 [2048, 512], P('seq')
- new_second: float32 [2048, 512], P('seq')
The draws below stay inside these ranges and needn't reach their ends.
All inputs are finite; a program needn't handle non-finite values.
Results may differ from the reference program's by a relative error of at most 0.02.
Values may be sent and summed in bfloat16 or wider, within the bound.
A program may use at most 64 MiB of HBM per device.

```python
import math
import jax
import jax.numpy as jnp
from jax import lax

DW = 2048
HQ = 16
HK = 4
DH = 128
WINDOW = 512
OPT_STEP = 10
TOK_DEV = 128
SEQ = 65536
QW = 2048
KVW = 512


def draw_queries(key, part):
    entries = jnp.clip(jax.random.normal(jax.random.fold_in(key, 1), (SEQ, HQ * DH), jnp.float32), -6.0, 6.0)
    return entries.astype(jnp.bfloat16)


def draw_key_rows(key, part):
    entries = jnp.clip(jax.random.normal(jax.random.fold_in(key, 2), (SEQ, HK * DH), jnp.float32), -6.0, 6.0)
    return entries.astype(jnp.bfloat16)


def strengthened(array, key, source, target, shards_of, factor):
    owner, partner = [(jnp.arange(array.shape[dim]) // (array.shape[dim] // shards_of)).reshape([-1 if axis == dim else 1 for axis in range(array.ndim)]) for dim in (source, target)]
    chosen = jax.random.permutation(key, shards_of)[partner]
    strong = (owner == chosen) | (owner == (partner + shards_of // 2) % shards_of)
    return jnp.where(strong, factor * array, array)


def block_scale(stream_key, dims, cuts, smallest, largest):
    level, own = 1.0, jax.random.fold_in(stream_key, 6)
    for position, parts in cuts:
        steps = jnp.exp(jax.random.uniform(jax.random.fold_in(own, position), (parts,), jnp.float32, smallest / len(cuts), largest / len(cuts)))
        level = level * jnp.repeat(steps, dims[position] // parts).reshape([-1 if axis == position else 1 for axis in range(len(dims))])
    return level


def gaussian(stream_key, shape, deviation, bound, cuts=(), held_as=jnp.bfloat16):
    level = block_scale(stream_key, shape, cuts, -0.22, 0.18) if cuts else 1.0
    array = jax.random.normal(stream_key, shape, jnp.float32) * deviation * level
    return jnp.minimum(jnp.maximum(array, -bound), bound).astype(held_as)


def bell_draw_with(own_key, shape, scale, reach, shards, heavy, kind=jnp.bfloat16):
    array = scale * jax.random.normal(own_key, shape, jnp.float32)
    if shards:
        array = array * block_scale(own_key, shape, shards, -0.22, 0.18)
    return jnp.clip(strengthened(array, jax.random.fold_in(own_key, 3), *heavy), -reach, reach).astype(kind)


def setup_inputs(seed: int = 0) -> dict:
    arg_keys = jax.random.split(jax.random.key(seed), 8)
    hidden = bell_draw_with(arg_keys[0], (SEQ, DW), 1.0, 24.0, ((0, 512),), (0, 1, 512, 6.0))
    queries = draw_queries(jax.random.fold_in(arg_keys[7], 71), 0)
    key_rows = draw_key_rows(jax.random.fold_in(arg_keys[7], 71), 0)
    grad_out = gaussian(arg_keys[3], (SEQ, QW), 1.0, 6.0, ((0, 512),))
    master_value = gaussian(arg_keys[4], (DW, KVW), DW ** -0.5, 0.125, ((0, 512),), jnp.float32)
    adam_first = gaussian(arg_keys[5], (DW, KVW), 2.0, 12.0, ((0, 512),), jnp.float32)
    adam_second = jnp.clip(jnp.exp(math.log(100.0) - 4.6051702 * jax.random.uniform(arg_keys[6], (DW, KVW), jnp.float32) ** block_scale(arg_keys[6], (DW, KVW), ((0, 512),), -0.2, 0.2)), 1.0, 100.0)
    return {"hidden": hidden, "queries": queries, "key_rows": key_rows, "grad_out": grad_out, "master_value": master_value, "adam_first": adam_first, "adam_second": adam_second}


beta_first = 0.9
beta_second = 0.95
learning = 0.001
decay_rate = 0.1
epsilon = 1e-08

def attend_block(query_blk, grad_blk, key_win, value_win, allowed):
    ratio = HQ // HK
    scale = 1.0 / math.sqrt(DH)
    count = query_blk.shape[0]
    out_parts, dq_parts, dk_parts, dv_parts = ([], [], [], [])
    for group in range(HK):
        low = group * ratio * DH
        high = (group + 1) * ratio * DH
        query_group = query_blk[:, low:high].reshape(count, ratio, DH).astype(jnp.float32)
        grad_group = grad_blk[:, low:high].reshape(count, ratio, DH).astype(jnp.float32)
        key_group = key_win[:, group * DH:(group + 1) * DH].astype(jnp.float32)
        value_group = value_win[:, group * DH:(group + 1) * DH].astype(jnp.float32)
        scores = jnp.einsum('trd,sd->trs', query_group, key_group) * scale
        scores = jnp.where(allowed[:, None, :], scores, -jnp.inf)
        top = lax.optimization_barrier(jnp.max(scores, axis=2, keepdims=True))
        expd = jnp.exp(scores - top)
        probs = expd / lax.optimization_barrier(jnp.sum(expd, axis=2, keepdims=True))
        probs_low = probs.astype(jnp.bfloat16)
        out_group = jnp.einsum('trs,sd->trd', probs_low.astype(jnp.float32), value_group).astype(jnp.bfloat16)
        delta = lax.optimization_barrier(jnp.sum(grad_group * out_group.astype(jnp.float32), axis=2, keepdims=True))
        dprob = jnp.einsum('trd,sd->trs', grad_group, value_group)
        dscore = (probs * (dprob - delta)).astype(jnp.bfloat16).astype(jnp.float32)
        dq_group = (jnp.einsum('trs,sd->trd', dscore, key_group) * scale).astype(jnp.bfloat16)
        dk_group = jnp.einsum('trs,trd->sd', dscore, query_group) * scale
        dv_group = jnp.einsum('trs,trd->sd', probs_low.astype(jnp.float32), grad_group)
        out_parts.append(out_group.reshape(count, ratio * DH))
        dq_parts.append(dq_group.reshape(count, ratio * DH))
        dk_parts.append(dk_group)
        dv_parts.append(dv_group)
    return (jnp.concatenate(out_parts, 1), jnp.concatenate(dq_parts, 1), jnp.concatenate(dk_parts, 1), jnp.concatenate(dv_parts, 1))

def reference(hidden, queries, key_rows, grad_out, master_value, adam_first, adam_second):
    seq_len = hidden.shape[0]
    width = key_rows.shape[1]
    weight_low = master_value.astype(jnp.bfloat16)
    values = jnp.dot(hidden, weight_low, preferred_element_type=jnp.float32).astype(jnp.bfloat16)
    pad_keys = jnp.concatenate([jnp.zeros((WINDOW, width), jnp.bfloat16), key_rows], 0)
    pad_values = jnp.concatenate([jnp.zeros((WINDOW, width), jnp.bfloat16), values], 0)
    span_rows = WINDOW + TOK_DEV
    offsets = jnp.arange(span_rows, dtype=jnp.int32) - WINDOW
    relative = jnp.arange(TOK_DEV, dtype=jnp.int32)[:, None] - offsets[None, :]
    blocks = seq_len // TOK_DEV

    def advance(carry, block):
        key_acc, value_acc = carry
        start = (block * TOK_DEV).astype(jnp.int32)
        query_blk = lax.dynamic_slice_in_dim(queries, start, TOK_DEV, 0)
        grad_blk = lax.dynamic_slice_in_dim(grad_out, start, TOK_DEV, 0)
        key_win = lax.dynamic_slice_in_dim(pad_keys, start, span_rows, 0)
        value_win = lax.dynamic_slice_in_dim(pad_values, start, span_rows, 0)
        allowed = (relative >= 0) & (relative < WINDOW) & (start + offsets >= 0)[None, :]
        out_blk, dq_blk, dk_win, dv_win = attend_block(query_blk, grad_blk, key_win, value_win, allowed)
        key_acc = lax.dynamic_update_slice_in_dim(key_acc, lax.dynamic_slice_in_dim(key_acc, start, span_rows, 0) + dk_win, start, 0)
        value_acc = lax.dynamic_update_slice_in_dim(value_acc, lax.dynamic_slice_in_dim(value_acc, start, span_rows, 0) + dv_win, start, 0)
        return ((key_acc, value_acc), (out_blk, dq_blk))
    zeros_acc = jnp.zeros((seq_len + WINDOW, width), jnp.float32)
    (key_acc, value_acc), (out_all, dq_all) = lax.scan(advance, (zeros_acc, zeros_acc), jnp.arange(blocks, dtype=jnp.int32))
    attention = out_all.reshape(seq_len, queries.shape[1])
    grad_queries = dq_all.reshape(seq_len, queries.shape[1])
    grad_keys = key_acc[WINDOW:].astype(jnp.bfloat16)
    d_value = value_acc[WINDOW:].astype(jnp.bfloat16)
    grad_hidden = lax.dot_general(d_value, weight_low, (((1,), (1,)), ((), ())), preferred_element_type=jnp.float32).astype(jnp.bfloat16)
    grad_weight = lax.dot_general(hidden, d_value, (((0,), (0,)), ((), ())), preferred_element_type=jnp.float32)
    new_first = beta_first * adam_first + (1.0 - beta_first) * grad_weight
    new_second = beta_second * adam_second + (1.0 - beta_second) * grad_weight * grad_weight
    first_hat = new_first / (1.0 - beta_first ** OPT_STEP)
    second_hat = new_second / (1.0 - beta_second ** OPT_STEP)
    new_master = master_value - learning * (first_hat / (jnp.sqrt(second_hat) + epsilon) + decay_rate * master_value)
    return (attention, grad_queries, grad_keys, grad_hidden, new_master, new_first, new_second)
```

```python
import math

import jax
import jax.numpy as jnp
from jax import lax
from jax.experimental import pallas as pl
from jax.experimental.pallas import tpu as pltpu
from jax.sharding import PartitionSpec as P

HQ = 16
HK = 4
DH = 128
WINDOW = 512
OPT_STEP = 10
TOK = 128
SCALE = 1.0 / math.sqrt(DH)

beta_first = 0.9
beta_second = 0.95
learning = 0.001
decay_rate = 0.1
epsilon = 1e-08

F32 = jnp.float32
BF16 = jnp.bfloat16
MESH = pl.DeviceIdType.MESH

NX, NZ, NY = 4, 16, 4
ZL = 8
HALF = 256
QHALF = 1024


def nt(a, b):
    return lax.dot_general(a, b, (((1,), (1,)), ((), ())), preferred_element_type=F32)


def nn(a, b):
    return lax.dot_general(a, b, (((1,), (0,)), ((), ())), preferred_element_type=F32)


def tn(a, b):
    return lax.dot_general(a, b, (((0,), (0,)), ((), ())), preferred_element_type=F32)


def aligned(value, multiple):
    return pl.multiple_of(value, multiple)


def kernel(
    hid_ref, q_ref, k_ref, go_ref, w_ref, m_ref, v_ref,
    o_out, dq_out, gk_out, gh_out, nw_out, nm_out, nv_out,
    hbuf, qbuf, gobuf, kw, vw, wsib, wz, w2, bias, perm, hp, ht, pbuf, dsbuf,
    dvw, dkw, dvs, dvr, dks, dkr, dksib, dksib_s, dval, dx,
    gbuf, r1a, r1b, s1a, s1b, r2, t2, z3, r3, gx, obuf, dqbuf,
    loc, sib_s, sib_r, k_s, k_r, v_s, v_r, dv_s, dv_r, dk_s, dk_r,
    ag1_s, ag1_r, ag2_s, ag2_r, ag3_s, ag3_r, rs1_s, rs1_r, rs2_s, rs2_r, rs3_s, rs3_r,
):
    ZH = NZ // ZL
    ROWS = ZL * 8
    PG = NY * ROWS
    NG = NX * ZH
    NCHIP = NX * NZ * NY
    d = lax.axis_index("seq")
    c = d % 2
    o = 1 - c
    n = d // 2
    y = n % NY
    z = (n // NY) % NZ
    x = n // (NY * NZ)

    def chip(step):
        return (n + step + NCHIP) % NCHIP

    def dev(x_, z_, y_):
        return ((x_ * NZ + z_) * NY + y_) * 2 + c

    sibling = n * 2 + o

    def remote(src, dst, ssem, rsem, device):
        return pltpu.make_async_remote_copy(
            src_ref=src, dst_ref=dst, send_sem=ssem, recv_sem=rsem,
            device_id=(device,), device_id_type=MESH,
        )

    def x_peer(k):
        return (x + k) % NX

    def y_peer(k):
        return (y + k) % NY

    barrier = pltpu.get_barrier_semaphore()

    def greet(device):
        pl.semaphore_signal(barrier, inc=1, device_id=(device,), device_id_type=MESH)

    greet(sibling)
    for step in (-2, -1, 1, 2):
        for h in range(2):
            greet(chip(step) * 2 + h)
    for k in range(1, NX):
        greet(dev(x_peer(k), z, y))
    for k in range(1, NY):
        greet(dev(x, z, y_peer(k)))

    @pl.loop(1, NZ)
    def _(k):
        greet(dev(x, (z + k) % NZ, y))

    pl.semaphore_wait(barrier, 1 + 8 + (NX - 1) + (NY - 1) + (NZ - 1))

    own_q = pl.ds(aligned(c * QHALF, QHALF), QHALF)
    oth_q = pl.ds(aligned(o * QHALF, QHALF), QHALF)
    own_k = pl.ds(aligned(c * HALF, HALF), HALF)
    oth_k = pl.ds(aligned(o * HALF, HALF), HALF)

    send_w = remote(w_ref.at[:, oth_k], wsib.at[c], sib_s.at[0], sib_r.at[0], sibling)
    send_w.start()
    k_sends = [remote(k_ref.at[:, oth_k], kw.at[4 + c], k_s.at[0], k_r.at[4 + c], sibling)]
    for step in (2, 1):
        for h in range(2):
            k_sends.append(
                remote(
                    k_ref.at[:, h * HALF : (h + 1) * HALF],
                    kw.at[(2 - step) * 2 + c],
                    k_s.at[len(k_sends)],
                    k_r.at[(2 - step) * 2 + c],
                    chip(step) * 2 + h,
                )
            )
    for copy in k_sends:
        copy.start()
    local = [
        pltpu.make_async_copy(k_ref.at[:, own_k], kw.at[4 + c], loc.at[0]),
        pltpu.make_async_copy(q_ref.at[:, own_q], qbuf.at[c], loc.at[1]),
        pltpu.make_async_copy(go_ref.at[:, own_q], gobuf.at[c], loc.at[2]),
        pltpu.make_async_copy(hid_ref, hbuf.at[c], loc.at[3]),
    ]
    for copy in local:
        copy.start()
    send_hid = remote(hid_ref, hbuf.at[c], sib_s.at[3], sib_r.at[3], sibling)
    send_q = remote(q_ref.at[:, oth_q], qbuf.at[c], sib_s.at[1], sib_r.at[1], sibling)
    send_go = remote(go_ref.at[:, oth_q], gobuf.at[c], sib_s.at[2], sib_r.at[2], sibling)
    for copy in (send_hid, send_q, send_go):
        copy.start()

    def arrived(dst, ssem, rsem):
        remote(dst, dst, ssem, rsem, sibling).wait_recv()

    wsib[c] = w_ref[:, own_k]
    arrived(wsib.at[o], sib_s.at[0], sib_r.at[0])
    block = jnp.concatenate([wsib[0], wsib[1]], 0)
    wz[z] = jnp.concatenate([block[:, :128], block[:, 128:]], 0).astype(BF16)

    def ag1(k):
        return remote(wz.at[z], wz.at[z], ag1_s.at[k], ag1_r.at[k], dev(x, (z + k) % NZ, y))

    @pl.loop(1, NZ)
    def _(k):
        ag1(k).start()

    row = lax.broadcasted_iota(jnp.int32, (TOK, 5 * TOK), 0)
    col = lax.broadcasted_iota(jnp.int32, (TOK, 5 * TOK), 1)
    relative = row + WINDOW - col
    for t in range(2):
        first = (d - c + t) * TOK - WINDOW
        allowed = (relative >= 0) & (relative < WINDOW) & (col + first >= 0)
        bias[t] = jnp.where(allowed, 0.0, -1e30).astype(F32)
    prow = lax.broadcasted_iota(jnp.int32, (PG, PG), 0)
    pcol = lax.broadcasted_iota(jnp.int32, (PG, PG), 1)
    source = ((prow % ROWS) // 8) * (NY * 8) + (prow // ROWS) * 8 + prow % 8
    perm[...] = jnp.where(source == pcol, 1.0, 0.0).astype(BF16)
    dvw[...] = jnp.zeros(dvw.shape, F32)
    dkw[...] = jnp.zeros(dkw.shape, F32)

    local[3].wait()
    arrived(hbuf.at[o], sib_s.at[3], sib_r.at[3])

    @pl.loop(0, NG)
    def _(g):
        cols = pl.ds(aligned(g * PG, PG), PG)
        both = jnp.concatenate([hbuf[0, :, cols], hbuf[1, :, cols]], 0)
        hp[g] = nt(both, perm[...]).astype(BF16)
        ht[g] = nt(perm[...], both).astype(BF16)

    @pl.loop(1, NZ)
    def _(k):
        slot = (z - k + NZ) % NZ
        remote(wz.at[slot], wz.at[slot], ag1_s.at[k], ag1_r.at[k], sibling).wait_recv()

    mine = pl.ds(x * ZH, ZH)
    for zh in range(ZH):
        rows = []
        for zl in range(ZL):
            block = wz[zh * ZL + zl].astype(F32)
            rows.append(jnp.concatenate([block[:8], block[8:]], 1))
        w2[c, x * ZH + zh, y] = jnp.concatenate(rows, 0).astype(BF16)

    def ag2_x(k, who):
        at = w2.at[c, pl.ds(who * ZH, ZH), y]
        return remote(at, at, ag2_s.at[k - 1], ag2_r.at[k - 1], dev(x_peer(k), z, y))

    def ag2_y(k, who):
        at = w2.at[c, mine, who]
        return remote(at, at, ag2_s.at[k - 1], ag2_r.at[k - 1], dev(x, z, y_peer(k)))

    def ag3_x(k, who):
        at = w2.at[c, pl.ds(who * ZH, ZH)]
        return remote(at, at, ag3_s.at[k - 1], ag3_r.at[k - 1], dev(x_peer(k), z, y))

    def ag3_y(k, who):
        at = w2.at[c, :, who]
        return remote(at, at, ag3_s.at[k - 1], ag3_r.at[k - 1], dev(x, z, y_peer(k)))

    @pl.when(c == 0)
    def _():
        for k in range(1, NY):
            ag2_y(k, y).start()

    @pl.when(c == 1)
    def _():
        for k in range(1, NX):
            ag2_x(k, x).start()

    for step in (2, 1):
        for h in range(2):
            slot = (2 - step) * 2 + h
            arrived(kw.at[slot], k_s.at[0], k_r.at[slot])
    arrived(kw.at[4 + o], k_s.at[0], k_r.at[4 + o])
    local[0].wait()
    local[1].wait()
    local[2].wait()
    arrived(qbuf.at[o], sib_s.at[1], sib_r.at[1])
    arrived(gobuf.at[o], sib_s.at[2], sib_r.at[2])

    @pl.when(c == 0)
    def _():
        for k in range(1, NY):
            ag2_y(k, (y - k + NY) % NY).wait_recv()
        for k in range(1, NX):
            ag3_x(k, x).start()

    @pl.when(c == 1)
    def _():
        for k in range(1, NX):
            ag2_x(k, (x - k + NX) % NX).wait_recv()
        for k in range(1, NY):
            ag3_y(k, y).start()

    @pl.loop(0, 4)
    def _(u):
        t = u // 2
        g = u % 2
        kc = pl.ds(aligned(g * DH, DH), DH)
        keys = kw[pl.ds(t, 5), :, kc].reshape(5 * TOK, DH)
        grads = []
        for r in range(4):
            qc = pl.ds(aligned(g * 512 + r * DH, DH), DH)
            s = nt(qbuf[t, :, qc], keys) + bias[t]
            top = jnp.max(s, axis=1, keepdims=True)
            e = jnp.exp2((s - top) * (SCALE * math.log2(math.e)))
            inv = 1.0 / jnp.sum(e, axis=1, keepdims=True)
            pbuf[u, r * TOK : (r + 1) * TOK, :] = (e * inv).astype(BF16)
            grads.append(gobuf[t, :, qc])
        dv = tn(pbuf[u], jnp.concatenate(grads, 0))
        dvw[pl.ds(t, 5), :, kc] += dv.reshape(5, TOK, DH)

    for j in range(4):
        dvs[j] = dvw[j].astype(BF16)
    dv_sends = [
        remote(dvs.at[pl.ds((2 - k) * 2, 2)], dvr.at[k - 1], dv_s.at[k - 1], dv_r.at[k - 1], chip(-k) * 2 + c)
        for k in (1, 2)
    ]
    dv_sends[1].start()
    dv_sends[0].start()

    @pl.when(c == 0)
    def _():
        for k in range(1, NX):
            ag3_x(k, (x - k + NX) % NX).wait_recv()

    @pl.when(c == 1)
    def _():
        for k in range(1, NY):
            ag3_y(k, (y - k + NY) % NY).wait_recv()

    values = jnp.zeros((2 * TOK, HALF), F32)
    for g in range(NG):
        values = values + nn(hp[g], w2[c, g].reshape(PG, HALF))
    values = values.astype(BF16)
    vw[4] = values[:TOK]
    vw[5] = values[TOK:]
    v_sends = [
        remote(vw.at[4:6], vw.at[pl.ds((2 - k) * 2, 2)], v_s.at[k - 1], v_r.at[k - 1], chip(k) * 2 + c)
        for k in (1, 2)
    ]
    v_sends[1].start()
    v_sends[0].start()
    send_w2 = remote(w2.at[c], w2.at[c], sib_s.at[4], sib_r.at[4], sibling)
    send_w2.start()

    for k in (1, 2):
        arrived(dvr.at[k - 1], dv_s.at[k - 1], dv_r.at[k - 1])
    total = dvw[4:6] + dvr[0].astype(F32) + dvr[1].astype(F32)
    dval[...] = total.astype(BF16)
    dx[c] = dval[c]
    send_dx = remote(dval.at[o], dx.at[c], sib_s.at[5], sib_r.at[5], sibling)
    send_dx.start()

    @pl.loop(0, NG)
    def _(g):
        gw = nn(ht[g], dval[...].reshape(2 * TOK, HALF))
        gbuf[g] = gw.astype(BF16).reshape(NY, ROWS, HALF)

    def rs1_x(k):
        return remote(
            gbuf.at[pl.ds(x_peer(k) * ZH, ZH)], r1a.at[k - 1], rs1_s.at[k - 1], rs1_r.at[k - 1],
            dev(x_peer(k), z, y),
        )

    def rs1_y(k):
        return remote(
            gbuf.at[:, y_peer(k)], r1b.at[k - 1], rs1_s.at[k - 1], rs1_r.at[k - 1], dev(x, z, y_peer(k))
        )

    def rs2_y(k):
        return remote(
            s1a.at[:, y_peer(k)], r2.at[k - 1], rs2_s.at[k - 1], rs2_r.at[k - 1], dev(x, z, y_peer(k))
        )

    def rs2_x(k):
        return remote(
            s1b.at[pl.ds(x_peer(k) * ZH, ZH)], r2.at[k - 1], rs2_s.at[k - 1], rs2_r.at[k - 1],
            dev(x_peer(k), z, y),
        )

    @pl.when(c == 0)
    def _():
        for k in range(1, NX):
            rs1_x(k).start()

    @pl.when(c == 1)
    def _():
        for k in range(1, NY):
            rs1_y(k).start()

    for k in (1, 2):
        at = vw.at[pl.ds((2 - k) * 2, 2)]
        arrived(at, v_s.at[k - 1], v_r.at[k - 1])

    def path_b(t):
        @pl.loop(0, 2)
        def _(g):
            u = t * 2 + g
            kc = pl.ds(aligned(g * DH, DH), DH)
            keys = kw[pl.ds(t, 5), :, kc].reshape(5 * TOK, DH)
            vals = vw[pl.ds(t, 5), :, kc].reshape(5 * TOK, DH)
            queries = []
            for r in range(4):
                qc = pl.ds(aligned(g * 512 + r * DH, DH), DH)
                p = pbuf[u, r * TOK : (r + 1) * TOK, :]
                go = gobuf[t, :, qc]
                out = nn(p, vals).astype(BF16)
                delta = jnp.sum(go.astype(F32) * out.astype(F32), axis=1, keepdims=True)
                ds = (p.astype(F32) * (nt(go, vals) - delta)).astype(BF16)
                obuf[t, :, qc] = out
                dqbuf[t, :, qc] = (nn(ds, keys) * SCALE).astype(BF16)
                dsbuf[r * TOK : (r + 1) * TOK, :] = ds
                queries.append(qbuf[t, :, qc])
            dk = tn(dsbuf[...], jnp.concatenate(queries, 0)) * SCALE
            dkw[pl.ds(t, 5), :, kc] += dk.reshape(5, TOK, DH)

    path_b(o)
    send_o = remote(obuf.at[o], o_out.at[:, own_q], sib_s.at[6], sib_r.at[6], sibling)
    send_dq = remote(dqbuf.at[o], dq_out.at[:, own_q], sib_s.at[7], sib_r.at[7], sibling)
    send_o.start()
    send_dq.start()
    path_b(c)
    for j in range(4):
        dks[j] = dkw[j].astype(BF16)
    dk_sends = []
    for k in (2, 1):
        for t in range(2):
            i = (k - 1) * 2
            dk_sends.append(
                remote(dks.at[(2 - k) * 2 + t], dkr.at[i + c], dk_s.at[i + t], dk_r.at[i + c], chip(-k) * 2 + t)
            )
    dksib_s[...] = dkw[4 + o]
    dk_sends.append(remote(dksib_s, dksib, dk_s.at[4], dk_r.at[4], sibling))
    for copy in dk_sends:
        copy.start()
    o_out[:, own_q] = obuf[c]
    dq_out[:, own_q] = dqbuf[c]

    @pl.when(c == 0)
    def _():
        for k in range(1, NX):
            arrived(r1a.at[k - 1], rs1_s.at[k - 1], rs1_r.at[k - 1])
        part = gbuf[pl.ds(x * ZH, ZH)].astype(F32)
        for k in range(1, NX):
            part = part + r1a[k - 1].astype(F32)
        s1a[...] = part.astype(BF16)
        for k in range(1, NY):
            rs2_y(k).start()

    @pl.when(c == 1)
    def _():
        for k in range(1, NY):
            arrived(r1b.at[k - 1], rs1_s.at[k - 1], rs1_r.at[k - 1])
        part = gbuf[:, y].astype(F32)
        for k in range(1, NY):
            part = part + r1b[k - 1].astype(F32)
        s1b[...] = part.astype(BF16)
        for k in range(1, NX):
            rs2_x(k).start()

    arrived(dx.at[o], sib_s.at[5], sib_r.at[5])
    arrived(w2.at[o], sib_s.at[4], sib_r.at[4])

    @pl.loop(0, NG)
    def _(g):
        both = nt(dx[0], w2[0, g].reshape(PG, HALF)) + nt(dx[1], w2[1, g].reshape(PG, HALF))
        gh_out[:, pl.ds(aligned(g * PG, PG), PG)] = nn(both.astype(BF16), perm[...]).astype(BF16)

    @pl.when(c == 0)
    def _():
        t2[...] = s1a[:, y].astype(F32)

    @pl.when(c == 1)
    def _():
        t2[...] = s1b[pl.ds(x * ZH, ZH)].astype(F32)

    for k in range(1, NX):
        arrived(r2.at[k - 1], rs2_s.at[k - 1], rs2_r.at[k - 1])
    part = t2[...]
    for k in range(1, NX):
        part = part + r2[k - 1].astype(F32)
    part = part.reshape(NZ, 8, HALF)
    for zz in range(NZ):
        z3[zz] = jnp.concatenate([part[zz, :, :128], part[zz, :, 128:]], 0).astype(BF16)

    def rs3(k):
        z_ = (z + k) % NZ
        return remote(z3.at[z_], r3.at[z], rs3_s.at[k], rs3_r.at[k], dev(x, z_, y))

    @pl.loop(1, NZ)
    def _(k):
        rs3(k).start()

    r3[z] = z3[z]

    for i in range(4):
        arrived(dkr.at[i], dk_s.at[i], dk_r.at[i])
    arrived(dksib, dk_s.at[4], dk_r.at[4])
    gk_out[:, own_k] = (dkw[4 + c] + dkr[c].astype(F32) + dkr[2 + c].astype(F32)).astype(BF16)
    gk_out[:, oth_k] = (dksib[...] + dkr[o].astype(F32) + dkr[2 + o].astype(F32)).astype(BF16)

    @pl.loop(1, NZ)
    def _(k):
        slot = (z - k + NZ) % NZ
        remote(r3.at[slot], r3.at[slot], rs3_s.at[k], rs3_r.at[k], sibling).wait_recv()

    acc = r3[0].astype(F32)
    for zz in range(1, NZ):
        acc = acc + r3[zz].astype(F32)
    gx[c] = jnp.concatenate([acc[:8], acc[8:]], 1)
    send_gx = remote(gx.at[c], gx.at[c], sib_s.at[8], sib_r.at[8], sibling)
    send_gx.start()
    arrived(gx.at[o], sib_s.at[8], sib_r.at[8])
    both = jnp.concatenate([gx[0], gx[1]], 1)
    grad = jnp.where(c == 0, both[:4], both[4:])
    first = beta_first * m_ref[...] + (1.0 - beta_first) * grad
    second = beta_second * v_ref[...] + (1.0 - beta_second) * grad * grad
    nm_out[...] = first
    nv_out[...] = second
    first_hat = first / (1.0 - beta_first**OPT_STEP)
    second_hat = second / (1.0 - beta_second**OPT_STEP)
    w = w_ref[...]
    nw_out[...] = w - learning * (first_hat / (jnp.sqrt(second_hat) + epsilon) + decay_rate * w)

    arrived(o_out.at[:, oth_q], sib_s.at[6], sib_r.at[6])
    arrived(dq_out.at[:, oth_q], sib_s.at[7], sib_r.at[7])
    for copy in [send_w, send_hid, send_q, send_go, send_w2, send_dx, send_o, send_dq, send_gx]:
        copy.wait_send()
    for copy in k_sends + dv_sends + v_sends + dk_sends:
        copy.wait_send()

    @pl.loop(1, NZ)
    def _(k):
        ag1(k).wait_send()
        rs3(k).wait_send()

    @pl.when(c == 0)
    def _():
        for k in range(1, NX):
            ag2_y(k, y).wait_send()
            ag3_x(k, x).wait_send()
            rs1_x(k).wait_send()
            rs2_y(k).wait_send()

    @pl.when(c == 1)
    def _():
        for k in range(1, NX):
            ag2_x(k, x).wait_send()
            ag3_y(k, y).wait_send()
            rs1_y(k).wait_send()
            rs2_x(k).wait_send()


def shards(hidden, queries, key_rows, grad_out, master_value, adam_first, adam_second):
    ZH = NZ // ZL
    ROWS = ZL * 8
    PG = NY * ROWS
    NG = NX * ZH
    V = pltpu.VMEM
    DMA = pltpu.SemaphoreType.DMA
    scratch = [
        V((2, TOK, NG * PG), BF16),
        V((2, TOK, QHALF), BF16),
        V((2, TOK, QHALF), BF16),
        V((6, TOK, HALF), BF16),
        V((6, TOK, HALF), BF16),
        V((2, 4, HALF), F32),
        V((NZ, 16, 128), BF16),
        V((2, NG, NY, ROWS, HALF), BF16),
        V((2, TOK, 5 * TOK), F32),
        V((PG, PG), BF16),
        V((NG, 2 * TOK, PG), BF16),
        V((NG, PG, 2 * TOK), BF16),
        V((4, 4 * TOK, 5 * TOK), BF16),
        V((4 * TOK, 5 * TOK), BF16),
        V((6, TOK, HALF), F32),
        V((6, TOK, HALF), F32),
        V((4, TOK, HALF), BF16),
        V((2, 2, TOK, HALF), BF16),
        V((4, TOK, HALF), BF16),
        V((4, TOK, HALF), BF16),
        V((TOK, HALF), F32),
        V((TOK, HALF), F32),
        V((2, TOK, HALF), BF16),
        V((2, TOK, HALF), BF16),
        V((NG, NY, ROWS, HALF), BF16),
        V((NX - 1, ZH, NY, ROWS, HALF), BF16),
        V((NY - 1, NG, ROWS, HALF), BF16),
        V((ZH, NY, ROWS, HALF), BF16),
        V((NG, ROWS, HALF), BF16),
        V((NX - 1, ZH, ROWS, HALF), BF16),
        V((ZH, ROWS, HALF), F32),
        V((NZ, 16, 128), BF16),
        V((NZ, 16, 128), BF16),
        V((2, 8, HALF), F32),
        V((2, TOK, QHALF), BF16),
        V((2, TOK, QHALF), BF16),
        DMA((4,)),
        DMA((9,)), DMA((9,)),
        DMA((5,)), DMA((6,)),
        DMA((2,)), DMA((2,)),
        DMA((2,)), DMA((2,)),
        DMA((5,)), DMA((5,)),
        DMA((NZ,)), DMA((NZ,)),
        DMA((NX - 1,)), DMA((NX - 1,)),
        DMA((NX - 1,)), DMA((NX - 1,)),
        DMA((NX - 1,)), DMA((NX - 1,)),
        DMA((NX - 1,)), DMA((NX - 1,)),
        DMA((NZ,)), DMA((NZ,)),
    ]
    any_ = pl.BlockSpec(memory_space=pl.ANY)
    vmem = pl.BlockSpec(memory_space=pltpu.VMEM)
    outs = (queries, queries, key_rows, hidden, master_value, adam_first, adam_second)
    return pl.pallas_call(
        kernel,
        out_shape=tuple(jax.ShapeDtypeStruct(a.shape, a.dtype) for a in outs),
        in_specs=[any_, any_, any_, any_, vmem, vmem, vmem],
        out_specs=(vmem,) * 7,
        scratch_shapes=scratch,
        compiler_params=pltpu.CompilerParams(
            collective_id=0, has_side_effects=True, vmem_limit_bytes=52 * 1024 * 1024
        ),
    )(hidden, queries, key_rows, grad_out, master_value, adam_first, adam_second)


def solution(mesh):
    placed = (P("seq", None),) * 7
    return jax.shard_map(
        shards, mesh=mesh, in_specs=placed, out_specs=placed, check_vma=False
    )
```

```python
import math

import jax
import jax.numpy as jnp
from jax import lax
from jax.experimental import pallas as pl
from jax.experimental.pallas import tpu as pltpu
from jax.sharding import PartitionSpec as P

HQ = 16
HK = 4
DH = 128
WINDOW = 512
OPT_STEP = 10
TOK = 128
SCALE = 1.0 / math.sqrt(DH)

beta_first = 0.9
beta_second = 0.95
learning = 0.001
decay_rate = 0.1
epsilon = 1e-08

F32 = jnp.float32
BF16 = jnp.bfloat16
MESH = pl.DeviceIdType.MESH

NX, NZ, NY = 4, 16, 4
ZL = 8
HALF = 256
QHALF = 1024


def nt(a, b):
    return lax.dot_general(a, b, (((1,), (1,)), ((), ())), preferred_element_type=F32)


def nn(a, b):
    return lax.dot_general(a, b, (((1,), (0,)), ((), ())), preferred_element_type=F32)


def tn(a, b):
    return lax.dot_general(a, b, (((0,), (0,)), ((), ())), preferred_element_type=F32)


def aligned(value, multiple):
    return pl.multiple_of(value, multiple)


def kernel(
    hid_ref, q_ref, k_ref, go_ref, w_ref, m_ref, v_ref,
    o_out, dq_out, gk_out, gh_out, nw_out, nm_out, nv_out,
    hbuf, qbuf, gobuf, kw, vw, wsib, wz, w2, bias, perm, hp, ht, pbuf, dsbuf,
    dvw, dkw, dvs, dvr, dks, dkr, dksib, dksib_s, dval, dx,
    gbuf, r1a, r1b, s1a, s1b, r2, t2, z3, r3, gx, obuf, dqbuf, adam, ghbuf,
    loc, sib_s, sib_r, k_s, k_r, v_s, v_r, dv_s, dv_r, dk_s, dk_r,
    ag1_s, ag1_r, ag2_s, ag2_r, ag3_s, ag3_r, rs1_s, rs1_r, rs2_s, rs2_r, rs3_s, rs3_r,
):
    ZH = NZ // ZL
    ROWS = ZL * 8
    PG = NY * ROWS
    NG = NX * ZH
    NCHIP = NX * NZ * NY
    d = lax.axis_index("seq")
    c = d % 2
    o = 1 - c
    n = d // 2
    y = n % NY
    z = (n // NY) % NZ
    x = n // (NY * NZ)

    def chip(step):
        return (n + step + NCHIP) % NCHIP

    def dev(x_, z_, y_):
        return ((x_ * NZ + z_) * NY + y_) * 2 + c

    sibling = n * 2 + o

    def remote(src, dst, ssem, rsem, device):
        return pltpu.make_async_remote_copy(
            src_ref=src, dst_ref=dst, send_sem=ssem, recv_sem=rsem,
            device_id=(device,), device_id_type=MESH,
        )

    def x_peer(k):
        return (x + k) % NX

    def y_peer(k):
        return (y + k) % NY

    pending = []

    def later(key, wait):
        pending.append((key, wait))

    def now(key):
        for item in [p for p in pending if p[0] == key]:
            item[1]()
            pending.remove(item)

    def go(copy, key):
        copy.start()
        later(key, copy.wait_recv)
        later("sent", copy.wait_send)

    def arrived(dst, ssem, rsem):
        remote(dst, dst, ssem, rsem, sibling).wait_recv()

    def on_core(which, act):
        @pl.when(c == which)
        def _():
            act()

    def along(key, zero, one):
        for which, (send, wait) in ((0, zero), (1, one)):
            def start(send=send):
                for k in (2, 1, 3) if NX == 4 else range(1, NX):
                    send(k).start()

            def got(wait=wait):
                for k in range(1, NX):
                    wait(k).wait_recv()

            def left(send=send):
                for k in range(1, NX):
                    send(k).wait_send()

            on_core(which, start)
            later(key, lambda which=which, act=got: on_core(which, act))
            later("sent", lambda which=which, act=left: on_core(which, act))

    def ring(key, send, wait):
        @pl.loop(0, NZ - 1)
        def _(i):
            far = (i + 1) // 2
            send(NZ // 2 + jnp.where(i % 2 == 0, far, -far)).start()

        def got():
            @pl.loop(1, NZ)
            def _(k):
                wait(k).wait_recv()

        def left():
            @pl.loop(1, NZ)
            def _(k):
                send(k).wait_send()

        later(key, got)
        later("sent", left)

    barrier = pltpu.get_barrier_semaphore()

    def greet(device):
        pl.semaphore_signal(barrier, inc=1, device_id=(device,), device_id_type=MESH)

    @pl.loop(0, NZ - 1)
    def _(i):
        far = (i + 1) // 2
        greet(dev(x, (z + NZ // 2 + jnp.where(i % 2 == 0, far, -far)) % NZ, y))

    for k in range(1, NX):
        greet(dev(x_peer(k), z, y))
    for k in range(1, NY):
        greet(dev(x, z, y_peer(k)))
    for step in (-2, -1, 1, 2):
        for h in range(2):
            greet(chip(step) * 2 + h)
    greet(sibling)

    own_q = pl.ds(aligned(c * QHALF, QHALF), QHALF)
    oth_q = pl.ds(aligned(o * QHALF, QHALF), QHALF)
    own_k = pl.ds(aligned(c * HALF, HALF), HALF)
    oth_k = pl.ds(aligned(o * HALF, HALF), HALF)

    for i, (key, src, dst) in enumerate(
        (
            ("w", w_ref.at[:, own_k], wsib.at[c]),
            ("k", k_ref.at[:, own_k], kw.at[4 + c]),
            ("q", q_ref.at[:, own_q], qbuf.at[c]),
            ("q", go_ref.at[:, own_q], gobuf.at[c]),
            ("hid", hid_ref, hbuf.at[c]),
            ("adam", w_ref, adam.at[0]),
            ("adam", m_ref, adam.at[1]),
            ("adam", v_ref, adam.at[2]),
        )
    ):
        copy = pltpu.make_async_copy(src, dst, loc.at[i])
        copy.start()
        later(key, copy.wait)

    row = lax.broadcasted_iota(jnp.int32, (TOK, 5 * TOK), 0)
    col = lax.broadcasted_iota(jnp.int32, (TOK, 5 * TOK), 1)
    relative = row + WINDOW - col
    for t in range(2):
        first = (d - c + t) * TOK - WINDOW
        allowed = (relative >= 0) & (relative < WINDOW) & (col + first >= 0)
        bias[t] = jnp.where(allowed, 0.0, -1e30).astype(F32)
    prow = lax.broadcasted_iota(jnp.int32, (PG, PG), 0)
    pcol = lax.broadcasted_iota(jnp.int32, (PG, PG), 1)
    source = ((prow % ROWS) // 8) * (NY * 8) + (prow // ROWS) * 8 + prow % 8
    perm[...] = jnp.where(source == pcol, 1.0, 0.0).astype(BF16)
    dvw[...] = jnp.zeros(dvw.shape, F32)
    dkw[...] = jnp.zeros(dkw.shape, F32)

    pl.semaphore_wait(barrier, 1 + 8 + (NX - 1) + (NY - 1) + (NZ - 1))

    go(remote(w_ref.at[:, oth_k], wsib.at[c], sib_s.at[0], sib_r.at[0], sibling), "w")
    go(remote(k_ref.at[:, oth_k], kw.at[4 + c], k_s.at[0], k_r.at[4 + c], sibling), "none")
    for i, (step, h) in enumerate(((1, 0), (1, 1), (2, 0), (2, 1))):
        slot = (2 - step) * 2 + c
        go(
            remote(
                k_ref.at[:, h * HALF : (h + 1) * HALF], kw.at[slot], k_s.at[1 + i], k_r.at[slot],
                chip(step) * 2 + h,
            ),
            "none",
        )
    pending[:] = [p for p in pending if p[0] != "none"]

    def keys_in():
        arrived(kw.at[4 + o], k_s.at[0], k_r.at[4 + o])
        for slot in (2, 3, 0, 1):
            arrived(kw.at[slot], k_s.at[0], k_r.at[slot])

    later("k", keys_in)
    go(remote(q_ref.at[:, oth_q], qbuf.at[c], sib_s.at[1], sib_r.at[1], sibling), "q")
    go(remote(go_ref.at[:, oth_q], gobuf.at[c], sib_s.at[2], sib_r.at[2], sibling), "q")
    go(remote(hid_ref, hbuf.at[c], sib_s.at[3], sib_r.at[3], sibling), "hid")

    now("w")
    block = jnp.concatenate([wsib[0], wsib[1]], 0)
    wz[z] = jnp.concatenate([block[:, :128], block[:, 128:]], 0).astype(BF16)

    def ag1(k):
        return remote(wz.at[z], wz.at[z], ag1_s.at[k], ag1_r.at[k], dev(x, (z + k) % NZ, y))

    def ag1_in(k):
        slot = (z - k + NZ) % NZ
        return remote(wz.at[slot], wz.at[slot], ag1_s.at[k], ag1_r.at[k], sibling)

    ring("ag1", ag1, ag1_in)

    def ag2_x(k, who):
        at = w2.at[c, pl.ds(who * ZH, ZH), y]
        return remote(at, at, ag2_s.at[k - 1], ag2_r.at[k - 1], dev(x_peer(k), z, y))

    def ag2_y(k, who):
        at = w2.at[c, pl.ds(x * ZH, ZH), who]
        return remote(at, at, ag2_s.at[k - 1], ag2_r.at[k - 1], dev(x, z, y_peer(k)))

    def ag3_x(k, who):
        at = w2.at[c, pl.ds(who * ZH, ZH)]
        return remote(at, at, ag3_s.at[k - 1], ag3_r.at[k - 1], dev(x_peer(k), z, y))

    def ag3_y(k, who):
        at = w2.at[c, :, who]
        return remote(at, at, ag3_s.at[k - 1], ag3_r.at[k - 1], dev(x, z, y_peer(k)))

    def gather_second():
        now("ag1")
        for zh in range(ZH):
            rows = []
            for zl in range(ZL):
                block = wz[zh * ZL + zl].astype(F32)
                rows.append(jnp.concatenate([block[:8], block[8:]], 1))
            w2[c, x * ZH + zh, y] = jnp.concatenate(rows, 0).astype(BF16)
        along(
            "ag2",
            (lambda k: ag2_y(k, y), lambda k: ag2_y(k, (y - k + NY) % NY)),
            (lambda k: ag2_x(k, x), lambda k: ag2_x(k, (x - k + NX) % NX)),
        )

    def gather_third():
        now("ag2")
        along(
            "ag3",
            (lambda k: ag3_x(k, x), lambda k: ag3_x(k, (x - k + NX) % NX)),
            (lambda k: ag3_y(k, y), lambda k: ag3_y(k, (y - k + NY) % NY)),
        )

    def path_a(t, g):
        keys = kw[pl.ds(t, 5), :, g * DH : (g + 1) * DH].reshape(5 * TOK, DH)
        grads = []
        for r in range(4):
            qc = slice(g * 512 + r * DH, g * 512 + (r + 1) * DH)
            s = nt(qbuf[t, :, qc], keys) + bias[t]
            top = jnp.max(s, axis=1, keepdims=True)
            e = jnp.exp2((s - top) * (SCALE * math.log2(math.e)))
            inv = 1.0 / jnp.sum(e, axis=1, keepdims=True)
            pbuf[t * 2 + g, r * TOK : (r + 1) * TOK, :] = (e * inv).astype(BF16)
            grads.append(gobuf[t, :, qc])
        dv = tn(pbuf[t * 2 + g], jnp.concatenate(grads, 0))
        dvw[pl.ds(t, 5), :, g * DH : (g + 1) * DH] += dv.reshape(5, TOK, DH)

    now("k")
    now("q")
    for g in range(2):
        @pl.loop(0, 2)
        def _(t):
            path_a(t, g)

        for j in range(4):
            dvs[g, j] = dvw[j, :, g * DH : (g + 1) * DH].astype(BF16)
        for k in (1, 2):
            i = g * 2 + k - 1
            go(
                remote(dvs.at[g, pl.ds((2 - k) * 2, 2)], dvr.at[i], dv_s.at[i], dv_r.at[i], chip(-k) * 2 + c),
                "dv",
            )
        if g == 0:
            gather_second()

    now("hid")

    def features(low, high):
        @pl.loop(low, high)
        def _(g):
            cols = pl.ds(aligned(g * PG, PG), PG)
            both = jnp.concatenate([hbuf[0, :, cols], hbuf[1, :, cols]], 0)
            hp[g] = nt(both, perm[...]).astype(BF16)
            ht[g] = nt(perm[...], both).astype(BF16)

    features(0, NG // 2)
    gather_third()
    features(NG // 2, NG)

    now("dv")
    for g in range(2):
        cols = slice(g * DH, (g + 1) * DH)
        total = dvw[4:6, :, cols] + dvr[g * 2].astype(F32) + dvr[g * 2 + 1].astype(F32)
        dval[:, :, cols] = total.astype(BF16)
    dx[c] = dval[c]
    go(remote(dval.at[o], dx.at[c], sib_s.at[5], sib_r.at[5], sibling), "dx")

    @pl.loop(0, NG)
    def _(g):
        gw = nn(ht[g], dval[...].reshape(2 * TOK, HALF))
        gbuf[g] = gw.astype(BF16).reshape(NY, ROWS, HALF)

    def rs1_x(k):
        return remote(
            gbuf.at[pl.ds(x_peer(k) * ZH, ZH)], r1a.at[k - 1], rs1_s.at[k - 1], rs1_r.at[k - 1],
            dev(x_peer(k), z, y),
        )

    def rs1_y(k):
        return remote(
            gbuf.at[:, y_peer(k)], r1b.at[k - 1], rs1_s.at[k - 1], rs1_r.at[k - 1], dev(x, z, y_peer(k))
        )

    def rs2_y(k):
        return remote(
            s1a.at[:, y_peer(k)], r2.at[k - 1], rs2_s.at[k - 1], rs2_r.at[k - 1], dev(x, z, y_peer(k))
        )

    def rs2_x(k):
        return remote(
            s1b.at[pl.ds(x_peer(k) * ZH, ZH)], r2.at[k - 1], rs2_s.at[k - 1], rs2_r.at[k - 1],
            dev(x_peer(k), z, y),
        )

    along("rs1", (rs1_x, rs1_x), (rs1_y, rs1_y))

    now("ag3")
    values = jnp.zeros((2 * TOK, HALF), F32)
    for g in range(NG):
        values = values + nn(hp[g], w2[c, g].reshape(PG, HALF))
    values = values.astype(BF16)
    vw[4] = values[:TOK]
    vw[5] = values[TOK:]
    for k in (1, 2):
        go(
            remote(vw.at[4:6], vw.at[pl.ds((2 - k) * 2, 2)], v_s.at[k - 1], v_r.at[k - 1], chip(k) * 2 + c),
            "none",
        )
        at = vw.at[pl.ds((2 - k) * 2, 2)]
        later("v", lambda at=at, k=k: arrived(at, v_s.at[k - 1], v_r.at[k - 1]))
    pending[:] = [p for p in pending if p[0] != "none"]
    go(remote(w2.at[c], w2.at[c], sib_s.at[4], sib_r.at[4], sibling), "none")
    pending[:] = [p for p in pending if p[0] != "none"]
    later("w2", lambda: arrived(w2.at[o], sib_s.at[4], sib_r.at[4]))

    now("dx")
    now("w2")

    @pl.loop(0, NG)
    def _(g):
        both = nt(dx[0], w2[0, g].reshape(PG, HALF)) + nt(dx[1], w2[1, g].reshape(PG, HALF))
        ghbuf[:, pl.ds(aligned(g * PG, PG), PG)] = nn(both.astype(BF16), perm[...]).astype(BF16)

    copy = pltpu.make_async_copy(ghbuf, gh_out, loc.at[10])
    copy.start()
    later("sent", copy.wait)

    now("rs1")

    def sum_zero():
        part = gbuf[pl.ds(x * ZH, ZH)].astype(F32)
        for k in range(1, NX):
            part = part + r1a[k - 1].astype(F32)
        s1a[...] = part.astype(BF16)
        t2[...] = s1a[:, y].astype(F32)

    def sum_one():
        part = gbuf[:, y].astype(F32)
        for k in range(1, NY):
            part = part + r1b[k - 1].astype(F32)
        s1b[...] = part.astype(BF16)
        t2[...] = s1b[pl.ds(x * ZH, ZH)].astype(F32)

    on_core(0, sum_zero)
    on_core(1, sum_one)
    along("rs2", (rs2_y, rs2_y), (rs2_x, rs2_x))

    def rs3(k):
        z_ = (z + k) % NZ
        return remote(z3.at[z_], r3.at[z], rs3_s.at[k], rs3_r.at[k], dev(x, z_, y))

    def rs3_in(k):
        slot = (z - k + NZ) % NZ
        return remote(r3.at[slot], r3.at[slot], rs3_s.at[k], rs3_r.at[k], sibling)

    def scatter_third():
        now("rs2")
        part = t2[...]
        for k in range(1, NX):
            part = part + r2[k - 1].astype(F32)
        part = part.reshape(NZ, 8, HALF)
        for zz in range(NZ):
            z3[zz] = jnp.concatenate([part[zz, :, :128], part[zz, :, 128:]], 0).astype(BF16)
        ring("rs3", rs3, rs3_in)
        r3[z] = z3[z]

    def path_b(t, g):
        keys = kw[pl.ds(t, 5), :, g * DH : (g + 1) * DH].reshape(5 * TOK, DH)
        vals = vw[pl.ds(t, 5), :, g * DH : (g + 1) * DH].reshape(5 * TOK, DH)
        queries = []
        for r in range(4):
            qc = slice(g * 512 + r * DH, g * 512 + (r + 1) * DH)
            p = pbuf[t * 2 + g, r * TOK : (r + 1) * TOK, :]
            grad = gobuf[t, :, qc]
            out = nn(p, vals).astype(BF16)
            delta = jnp.sum(grad.astype(F32) * out.astype(F32), axis=1, keepdims=True)
            ds = (p.astype(F32) * (nt(grad, vals) - delta)).astype(BF16)
            obuf[t, :, qc] = out
            dqbuf[t, :, qc] = (nn(ds, keys) * SCALE).astype(BF16)
            dsbuf[r * TOK : (r + 1) * TOK, :] = ds
            queries.append(qbuf[t, :, qc])
        dk = tn(dsbuf[...], jnp.concatenate(queries, 0)) * SCALE
        dkw[pl.ds(t, 5), :, g * DH : (g + 1) * DH] += dk.reshape(5, TOK, DH)

    now("v")
    for g in range(2):
        cols = slice(g * DH, (g + 1) * DH)

        @pl.loop(0, 2)
        def _(t):
            path_b(t, g)

        if g == 0:
            scatter_third()
        for j in range(4):
            dks[g, j] = dkw[j, :, cols].astype(BF16)
        dksib_s[g] = dkw[4 + o, :, cols]
        for k in (1, 2):
            for t in range(2):
                i = g * 4 + (k - 1) * 2
                copy = remote(
                    dks.at[g, (2 - k) * 2 + t], dkr.at[i + c], dk_s.at[i + t], dk_r.at[i + c], chip(-k) * 2 + t
                )
                copy.start()
                later("sent", copy.wait_send)
        go(remote(dksib_s.at[g], dksib.at[g], dk_s.at[8 + g], dk_r.at[8 + g], sibling), "dk")
        for i in range(g * 4, g * 4 + 4):
            later("dk", lambda i=i: arrived(dkr.at[i], dk_s.at[i], dk_r.at[i]))

    for i, (buf, out) in enumerate(((obuf, o_out), (dqbuf, dq_out))):
        go(remote(buf.at[o], out.at[:, own_q], sib_s.at[6 + i], sib_r.at[6 + i], sibling), "none")
        pending[:] = [p for p in pending if p[0] != "none"]
        at = out.at[:, oth_q]
        later("out", lambda i=i, at=at: arrived(at, sib_s.at[6 + i], sib_r.at[6 + i]))
        copy = pltpu.make_async_copy(buf.at[c], out.at[:, own_q], loc.at[8 + i])
        copy.start()
        later("sent", copy.wait)

    now("dk")
    for g in range(2):
        own = dkw[4 + c, :, g * DH : (g + 1) * DH]
        own = own + dkr[g * 4 + c].astype(F32) + dkr[g * 4 + 2 + c].astype(F32)
        oth = dksib[g] + dkr[g * 4 + o].astype(F32) + dkr[g * 4 + 2 + o].astype(F32)
        gk_out[:, pl.ds(aligned(c * HALF + g * DH, DH), DH)] = own.astype(BF16)
        gk_out[:, pl.ds(aligned(o * HALF + g * DH, DH), DH)] = oth.astype(BF16)

    now("rs3")
    acc = r3[0].astype(F32)
    for zz in range(1, NZ):
        acc = acc + r3[zz].astype(F32)
    gx[c] = jnp.concatenate([acc[:8], acc[8:]], 1)
    go(remote(gx.at[c], gx.at[c], sib_s.at[8], sib_r.at[8], sibling), "none")
    pending[:] = [p for p in pending if p[0] != "none"]
    now("adam")
    arrived(gx.at[o], sib_s.at[8], sib_r.at[8])
    both = jnp.concatenate([gx[0], gx[1]], 1)
    grad = jnp.where(c == 0, both[:4], both[4:])
    first = beta_first * adam[1] + (1.0 - beta_first) * grad
    second = beta_second * adam[2] + (1.0 - beta_second) * grad * grad
    nm_out[...] = first
    nv_out[...] = second
    first_hat = first / (1.0 - beta_first**OPT_STEP)
    second_hat = second / (1.0 - beta_second**OPT_STEP)
    w = adam[0]
    nw_out[...] = w - learning * (first_hat / (jnp.sqrt(second_hat) + epsilon) + decay_rate * w)

    for key, wait in pending:
        wait()


def settle(*refs):
    sems = refs[-1]
    copies = [pltpu.make_async_copy(refs[i], refs[7 + i], sems.at[i]) for i in range(7)]
    for copy in copies:
        copy.start()
    for copy in copies:
        copy.wait()


def shards(hidden, queries, key_rows, grad_out, master_value, adam_first, adam_second):
    ZH = NZ // ZL
    ROWS = ZL * 8
    PG = NY * ROWS
    NG = NX * ZH
    V = pltpu.VMEM
    DMA = pltpu.SemaphoreType.DMA
    scratch = [
        V((2, TOK, NG * PG), BF16),
        V((2, TOK, QHALF), BF16),
        V((2, TOK, QHALF), BF16),
        V((6, TOK, HALF), BF16),
        V((6, TOK, HALF), BF16),
        V((2, 4, HALF), F32),
        V((NZ, 16, 128), BF16),
        V((2, NG, NY, ROWS, HALF), BF16),
        V((2, TOK, 5 * TOK), F32),
        V((PG, PG), BF16),
        V((NG, 2 * TOK, PG), BF16),
        V((NG, PG, 2 * TOK), BF16),
        V((4, 4 * TOK, 5 * TOK), BF16),
        V((4 * TOK, 5 * TOK), BF16),
        V((6, TOK, HALF), F32),
        V((6, TOK, HALF), F32),
        V((2, 4, TOK, DH), BF16),
        V((4, 2, TOK, DH), BF16),
        V((2, 4, TOK, DH), BF16),
        V((8, TOK, DH), BF16),
        V((2, TOK, DH), F32),
        V((2, TOK, DH), F32),
        V((2, TOK, HALF), BF16),
        V((2, TOK, HALF), BF16),
        V((NG, NY, ROWS, HALF), BF16),
        V((NX - 1, ZH, NY, ROWS, HALF), BF16),
        V((NY - 1, NG, ROWS, HALF), BF16),
        V((ZH, NY, ROWS, HALF), BF16),
        V((NG, ROWS, HALF), BF16),
        V((NX - 1, ZH, ROWS, HALF), BF16),
        V((ZH, ROWS, HALF), F32),
        V((NZ, 16, 128), BF16),
        V((NZ, 16, 128), BF16),
        V((2, 8, HALF), F32),
        V((2, TOK, QHALF), BF16),
        V((2, TOK, QHALF), BF16),
        V((3, 4, 2 * HALF), F32),
        V((TOK, NG * PG), BF16),
        DMA((11,)),
        DMA((9,)), DMA((9,)),
        DMA((5,)), DMA((6,)),
        DMA((2,)), DMA((2,)),
        DMA((4,)), DMA((4,)),
        DMA((10,)), DMA((10,)),
        DMA((NZ,)), DMA((NZ,)),
        DMA((NX - 1,)), DMA((NX - 1,)),
        DMA((NX - 1,)), DMA((NX - 1,)),
        DMA((NX - 1,)), DMA((NX - 1,)),
        DMA((NX - 1,)), DMA((NX - 1,)),
        DMA((NZ,)), DMA((NZ,)),
    ]
    hbm = pl.BlockSpec(memory_space=pltpu.HBM)
    anywhere = pl.BlockSpec(memory_space=pl.ANY)
    vmem = pl.BlockSpec(memory_space=pltpu.VMEM)
    outs = (queries, queries, key_rows, hidden, master_value, adam_first, adam_second)
    shapes = tuple(jax.ShapeDtypeStruct(a.shape, a.dtype) for a in outs)
    results = pl.pallas_call(
        kernel,
        out_shape=shapes,
        in_specs=[hbm] * 7,
        out_specs=(anywhere, anywhere, vmem, anywhere, vmem, vmem, vmem),
        scratch_shapes=scratch,
        compiler_params=pltpu.CompilerParams(
            collective_id=0, has_side_effects=True, vmem_limit_bytes=52 * 1024 * 1024
        ),
    )(
        *(
            pltpu.with_memory_space_constraint(a, pltpu.HBM)
            for a in (hidden, queries, key_rows, grad_out, master_value, adam_first, adam_second)
        )
    )
    return pl.pallas_call(
        settle,
        out_shape=shapes,
        in_specs=[anywhere] * 7,
        out_specs=(hbm,) * 7,
        scratch_shapes=[DMA((7,))],
        compiler_params=pltpu.CompilerParams(vmem_limit_bytes=2 * 1024 * 1024),
    )(*results)


def solution(mesh):
    placed = (P("seq", None),) * 7
    return jax.shard_map(
        shards, mesh=mesh, in_specs=placed, out_specs=placed, check_vma=False
    )
```

```python
import functools
import math

import jax
import jax.numpy as jnp
from jax import lax
from jax.experimental import pallas as pl
from jax.experimental.pallas import tpu as pltpu
from jax.sharding import PartitionSpec as P

HQ = 16
HK = 4
DH = 128
WINDOW = 512
OPT_STEP = 10
TOK = 128
SCALE = 1.0 / math.sqrt(DH)

beta_first = 0.9
beta_second = 0.95
learning = 0.001
decay_rate = 0.1
epsilon = 1e-08

F32 = jnp.float32
BF16 = jnp.bfloat16
MESH = pl.DeviceIdType.MESH

NX, NZ, NY = 4, 16, 4
ZL = 8
HALF = 256
QHALF = 1024


def nt(a, b):
    return lax.dot_general(a, b, (((1,), (1,)), ((), ())), preferred_element_type=F32)


def nn(a, b):
    return lax.dot_general(a, b, (((1,), (0,)), ((), ())), preferred_element_type=F32)


def tn(a, b):
    return lax.dot_general(a, b, (((0,), (0,)), ((), ())), preferred_element_type=F32)


def aligned(value, multiple):
    return pl.multiple_of(value, multiple)


def kernel(
    hid_ref, q_ref, k_ref, go_ref, w_ref, m_ref, v_ref,
    o_out, dq_out, gk_out, gh_out, nw_out, nm_out, nv_out,
    hbuf, qbuf, gobuf, kw, vw, wsib, wz, w2, bias, perm, hp, ht, pbuf, dsbuf,
    dvw, dkw, dvs, dvr, dks, dkr, dksib, dksib_s, dval, dx,
    gbuf, r1a, r1b, s1a, s1b, r2, t2, z3, r3, gx, obuf, dqbuf, adam, ghbuf,
    loc, sib_s, sib_r, k_s, k_r, v_s, v_r, dv_s, dv_r, dk_s, dk_r,
    ag1_s, ag1_r, ag2_s, ag2_r, ag3_s, ag3_r, rs1_s, rs1_r, rs2_s, rs2_r, rs3_s, rs3_r,
):
    ZH = NZ // ZL
    ROWS = ZL * 8
    PG = NY * ROWS
    NG = NX * ZH
    NCHIP = NX * NZ * NY
    d = lax.axis_index("seq")
    c = d % 2
    o = 1 - c
    n = d // 2
    y = n % NY
    z = (n // NY) % NZ
    x = n // (NY * NZ)

    def chip(step):
        return (n + step + NCHIP) % NCHIP

    def dev(x_, z_, y_):
        return ((x_ * NZ + z_) * NY + y_) * 2 + c

    sibling = n * 2 + o

    def remote(src, dst, ssem, rsem, device):
        return pltpu.make_async_remote_copy(
            src_ref=src, dst_ref=dst, send_sem=ssem, recv_sem=rsem,
            device_id=(device,), device_id_type=MESH,
        )

    def x_peer(k):
        return (x + k) % NX

    def y_peer(k):
        return (y + k) % NY

    pending = []

    def later(key, wait):
        pending.append((key, wait))

    def now(key):
        for item in [p for p in pending if p[0] == key]:
            item[1]()
            pending.remove(item)

    def go(copy, key):
        copy.start()
        later(key, copy.wait_recv)
        later("sent", copy.wait_send)

    def arrived(dst, ssem, rsem):
        remote(dst, dst, ssem, rsem, sibling).wait_recv()

    def on_core(which, act):
        @pl.when(c == which)
        def _():
            act()

    def along(key, zero, one):
        for which, (send, wait) in ((0, zero), (1, one)):
            def start(send=send):
                for k in (2, 1, 3) if NX == 4 else range(1, NX):
                    send(k).start()

            def got(wait=wait):
                for k in range(1, NX):
                    wait(k).wait_recv()

            def left(send=send):
                for k in range(1, NX):
                    send(k).wait_send()

            on_core(which, start)
            later(key, lambda which=which, act=got: on_core(which, act))
            later("sent", lambda which=which, act=left: on_core(which, act))

    def ring(key, send, wait):
        @pl.loop(0, NZ - 1)
        def _(i):
            far = (i + 1) // 2
            send(NZ // 2 + jnp.where(i % 2 == 0, far, -far)).start()

        def got():
            @pl.loop(1, NZ)
            def _(k):
                wait(k).wait_recv()

        def left():
            @pl.loop(1, NZ)
            def _(k):
                send(k).wait_send()

        later(key, got)
        later("sent", left)

    barrier = pltpu.get_barrier_semaphore()

    def greet(device):
        pl.semaphore_signal(barrier, inc=1, device_id=(device,), device_id_type=MESH)

    @pl.loop(0, NZ - 1)
    def _(i):
        far = (i + 1) // 2
        greet(dev(x, (z + NZ // 2 + jnp.where(i % 2 == 0, far, -far)) % NZ, y))

    for k in range(1, NX):
        greet(dev(x_peer(k), z, y))
    for k in range(1, NY):
        greet(dev(x, z, y_peer(k)))
    for step in (-2, -1, 1, 2):
        for h in range(2):
            greet(chip(step) * 2 + h)
    greet(sibling)

    own_q = pl.ds(aligned(c * QHALF, QHALF), QHALF)
    oth_q = pl.ds(aligned(o * QHALF, QHALF), QHALF)
    own_k = pl.ds(aligned(c * HALF, HALF), HALF)
    oth_k = pl.ds(aligned(o * HALF, HALF), HALF)

    for i, (key, src, dst) in enumerate(
        (
            ("w", w_ref.at[:, own_k], wsib.at[c]),
            ("k", k_ref.at[:, own_k], kw.at[4 + c]),
            ("q", q_ref.at[:, own_q], qbuf.at[c]),
            ("q", go_ref.at[:, own_q], gobuf.at[c]),
            ("hid", hid_ref, hbuf.at[c]),
            ("adam", w_ref, adam.at[0]),
            ("adam", m_ref, adam.at[1]),
            ("adam", v_ref, adam.at[2]),
        )
    ):
        copy = pltpu.make_async_copy(src, dst, loc.at[i])
        copy.start()
        later(key, copy.wait)

    row = lax.broadcasted_iota(jnp.int32, (TOK, 5 * TOK), 0)
    col = lax.broadcasted_iota(jnp.int32, (TOK, 5 * TOK), 1)
    relative = row + WINDOW - col
    for t in range(2):
        first = (d - c + t) * TOK - WINDOW
        allowed = (relative >= 0) & (relative < WINDOW) & (col + first >= 0)
        bias[t] = jnp.where(allowed, 0.0, -1e30).astype(F32)
    prow = lax.broadcasted_iota(jnp.int32, (PG, PG), 0)
    pcol = lax.broadcasted_iota(jnp.int32, (PG, PG), 1)
    source = ((prow % ROWS) // 8) * (NY * 8) + (prow // ROWS) * 8 + prow % 8
    perm[...] = jnp.where(source == pcol, 1.0, 0.0).astype(BF16)
    dvw[...] = jnp.zeros(dvw.shape, F32)
    dkw[...] = jnp.zeros(dkw.shape, F32)

    pl.semaphore_wait(barrier, 1 + 8 + (NX - 1) + (NY - 1) + (NZ - 1))

    go(remote(w_ref.at[:, oth_k], wsib.at[c], sib_s.at[0], sib_r.at[0], sibling), "w")
    go(remote(k_ref.at[:, oth_k], kw.at[4 + c], k_s.at[0], k_r.at[4 + c], sibling), "none")
    for i, (step, h) in enumerate(((1, 0), (1, 1), (2, 0), (2, 1))):
        slot = (2 - step) * 2 + c
        go(
            remote(
                k_ref.at[:, h * HALF : (h + 1) * HALF], kw.at[slot], k_s.at[1 + i], k_r.at[slot],
                chip(step) * 2 + h,
            ),
            "none",
        )
    pending[:] = [p for p in pending if p[0] != "none"]

    def keys_in():
        arrived(kw.at[4 + o], k_s.at[0], k_r.at[4 + o])
        for slot in (2, 3, 0, 1):
            arrived(kw.at[slot], k_s.at[0], k_r.at[slot])

    later("k", keys_in)
    go(remote(q_ref.at[:, oth_q], qbuf.at[c], sib_s.at[1], sib_r.at[1], sibling), "q")
    go(remote(go_ref.at[:, oth_q], gobuf.at[c], sib_s.at[2], sib_r.at[2], sibling), "q")
    go(remote(hid_ref, hbuf.at[c], sib_s.at[3], sib_r.at[3], sibling), "hid")

    now("w")
    block = jnp.concatenate([wsib[0], wsib[1]], 0)
    wz[z] = jnp.concatenate([block[:, :128], block[:, 128:]], 0).astype(BF16)

    def ag1(k):
        return remote(wz.at[z], wz.at[z], ag1_s.at[k], ag1_r.at[k], dev(x, (z + k) % NZ, y))

    def ag1_in(k):
        slot = (z - k + NZ) % NZ
        return remote(wz.at[slot], wz.at[slot], ag1_s.at[k], ag1_r.at[k], sibling)

    ring("ag1", ag1, ag1_in)

    def ag2_x(k, who):
        at = w2.at[c, pl.ds(who * ZH, ZH), y]
        return remote(at, at, ag2_s.at[k - 1], ag2_r.at[k - 1], dev(x_peer(k), z, y))

    def ag2_y(k, who):
        at = w2.at[c, pl.ds(x * ZH, ZH), who]
        return remote(at, at, ag2_s.at[k - 1], ag2_r.at[k - 1], dev(x, z, y_peer(k)))

    def ag3_x(j, k, who):
        at = w2.at[c, pl.ds(who * ZH, ZH), (y - j + NY) % NY]
        i = j * (NX - 1) + k - 1
        return remote(at, at, ag3_s.at[i], ag3_r.at[i], dev(x_peer(k), z, y))

    def ag3_y(j, k, who):
        at = w2.at[c, pl.ds(((x - j + NX) % NX) * ZH, ZH), who]
        i = j * (NX - 1) + k - 1
        return remote(at, at, ag3_s.at[i], ag3_r.at[i], dev(x, z, y_peer(k)))

    def gather_third(j):
        along(
            "ag3",
            (lambda k: ag3_x(j, k, x), lambda k: ag3_x(j, k, (x - k + NX) % NX)),
            (lambda k: ag3_y(j, k, y), lambda k: ag3_y(j, k, (y - k + NY) % NY)),
        )

    def gather_second():
        now("ag1")
        for zh in range(ZH):
            rows = []
            for zl in range(ZL):
                block = wz[zh * ZL + zl].astype(F32)
                rows.append(jnp.concatenate([block[:8], block[8:]], 1))
            w2[c, x * ZH + zh, y] = jnp.concatenate(rows, 0).astype(BF16)
        along(
            "ag2",
            (lambda k: ag2_y(k, y), lambda k: ag2_y(k, (y - k + NY) % NY)),
            (lambda k: ag2_x(k, x), lambda k: ag2_x(k, (x - k + NX) % NX)),
        )
        gather_third(0)

    def path_a(t, g):
        keys = kw[pl.ds(t, 5), :, g * DH : (g + 1) * DH].reshape(5 * TOK, DH)
        grads = []
        for r in range(4):
            qc = slice(g * 512 + r * DH, g * 512 + (r + 1) * DH)
            s = nt(qbuf[t, :, qc], keys) + bias[t]
            top = jnp.max(s, axis=1, keepdims=True)
            e = jnp.exp2((s - top) * (SCALE * math.log2(math.e)))
            inv = 1.0 / jnp.sum(e, axis=1, keepdims=True)
            pbuf[t * 2 + g, r * TOK : (r + 1) * TOK, :] = (e * inv).astype(BF16)
            grads.append(gobuf[t, :, qc])
        dv = tn(pbuf[t * 2 + g], jnp.concatenate(grads, 0))
        dvw[pl.ds(t, 5), :, g * DH : (g + 1) * DH] += dv.reshape(5, TOK, DH)

    gather_second()
    now("k")
    now("q")
    for g in range(2):
        @pl.loop(0, 2)
        def _(t):
            path_a(t, g)

        for j in range(4):
            dvs[g, j] = dvw[j, :, g * DH : (g + 1) * DH].astype(BF16)
        for k in (1, 2):
            i = g * 2 + k - 1
            go(
                remote(dvs.at[g, pl.ds((2 - k) * 2, 2)], dvr.at[i], dv_s.at[i], dv_r.at[i], chip(-k) * 2 + c),
                "dv%d" % g,
            )

    now("ag2")
    for j in range(1, NY):
        gather_third(j)

    now("hid")

    @pl.loop(0, NG)
    def _(g):
        cols = pl.ds(aligned(g * PG, PG), PG)
        both = jnp.concatenate([hbuf[0, :, cols], hbuf[1, :, cols]], 0)
        hp[g] = nt(both, perm[...]).astype(BF16)
        ht[g] = nt(perm[...], both).astype(BF16)

    def rs1_x(g, k):
        low = slice(g * DH, (g + 1) * DH)
        i = g * (NX - 1) + k - 1
        return remote(
            gbuf.at[pl.ds(x_peer(k) * ZH, ZH), :, :, low], r1a.at[k - 1, :, :, :, low], rs1_s.at[i], rs1_r.at[i],
            dev(x_peer(k), z, y),
        )

    def rs1_y(g, k):
        low = slice(g * DH, (g + 1) * DH)
        i = g * (NX - 1) + k - 1
        return remote(
            gbuf.at[:, y_peer(k), :, low], r1b.at[k - 1, :, :, low], rs1_s.at[i], rs1_r.at[i],
            dev(x, z, y_peer(k)),
        )

    for g in range(2):
        now("dv%d" % g)
        low = slice(g * DH, (g + 1) * DH)
        total = dvw[4:6, :, low] + dvr[g * 2].astype(F32) + dvr[g * 2 + 1].astype(F32)
        dval[:, :, low] = total.astype(BF16)

        @pl.loop(0, NG)
        def _(f):
            gw = nn(ht[f], dval[:, :, low].reshape(2 * TOK, DH))
            gbuf[f, :, :, low] = gw.astype(BF16).reshape(NY, ROWS, DH)

        pair_x = functools.partial(rs1_x, g)
        pair_y = functools.partial(rs1_y, g)
        along("rs1", (pair_x, pair_x), (pair_y, pair_y))

    dx[c] = dval[c]
    go(remote(dval.at[o], dx.at[c], sib_s.at[5], sib_r.at[5], sibling), "dx")

    def rs2_y(k):
        return remote(
            s1a.at[:, y_peer(k)], r2.at[k - 1], rs2_s.at[k - 1], rs2_r.at[k - 1], dev(x, z, y_peer(k))
        )

    def rs2_x(k):
        return remote(
            s1b.at[pl.ds(x_peer(k) * ZH, ZH)], r2.at[k - 1], rs2_s.at[k - 1], rs2_r.at[k - 1],
            dev(x_peer(k), z, y),
        )

    now("ag3")
    values = jnp.zeros((2 * TOK, HALF), F32)
    for g in range(NG):
        values = values + nn(hp[g], w2[c, g].reshape(PG, HALF))
    values = values.astype(BF16)
    vw[4] = values[:TOK]
    vw[5] = values[TOK:]
    for g in range(2):
        low = slice(g * DH, (g + 1) * DH)
        for k in (1, 2):
            i = g * 2 + k - 1
            at = vw.at[pl.ds((2 - k) * 2, 2), :, low]
            copy = remote(vw.at[4:6, :, low], at, v_s.at[i], v_r.at[i], chip(k) * 2 + c)
            copy.start()
            later("sent", copy.wait_send)
            later("v%d" % g, lambda at=at, i=i: arrived(at, v_s.at[i], v_r.at[i]))
    go(remote(w2.at[c], w2.at[c], sib_s.at[4], sib_r.at[4], sibling), "none")
    pending[:] = [p for p in pending if p[0] != "none"]
    later("w2", lambda: arrived(w2.at[o], sib_s.at[4], sib_r.at[4]))

    now("rs1")

    def sum_zero():
        part = gbuf[pl.ds(x * ZH, ZH)].astype(F32)
        for k in range(1, NX):
            part = part + r1a[k - 1].astype(F32)
        s1a[...] = part.astype(BF16)
        t2[...] = s1a[:, y].astype(F32)

    def sum_one():
        part = gbuf[:, y].astype(F32)
        for k in range(1, NY):
            part = part + r1b[k - 1].astype(F32)
        s1b[...] = part.astype(BF16)
        t2[...] = s1b[pl.ds(x * ZH, ZH)].astype(F32)

    on_core(0, sum_zero)
    on_core(1, sum_one)
    along("rs2", (rs2_y, rs2_y), (rs2_x, rs2_x))

    def rs3(k):
        z_ = (z + k) % NZ
        return remote(z3.at[z_], r3.at[z], rs3_s.at[k], rs3_r.at[k], dev(x, z_, y))

    def rs3_in(k):
        slot = (z - k + NZ) % NZ
        return remote(r3.at[slot], r3.at[slot], rs3_s.at[k], rs3_r.at[k], sibling)

    def scatter_third():
        now("rs2")
        part = t2[...]
        for k in range(1, NX):
            part = part + r2[k - 1].astype(F32)
        part = part.reshape(NZ, 8, HALF)
        for zz in range(NZ):
            z3[zz] = jnp.concatenate([part[zz, :, :128], part[zz, :, 128:]], 0).astype(BF16)
        ring("rs3", rs3, rs3_in)
        r3[z] = z3[z]

    now("dx")
    now("w2")

    @pl.loop(0, NG)
    def _(g):
        both = nt(dx[0], w2[0, g].reshape(PG, HALF)) + nt(dx[1], w2[1, g].reshape(PG, HALF))
        ghbuf[:, pl.ds(aligned(g * PG, PG), PG)] = nn(both.astype(BF16), perm[...]).astype(BF16)

    copy = pltpu.make_async_copy(ghbuf, gh_out, loc.at[10])
    copy.start()
    later("sent", copy.wait)

    def stacked(ref, t, g):
        return jnp.concatenate([ref[t, :, g * 512 + r * DH : g * 512 + (r + 1) * DH] for r in range(4)], 0)

    def path_b(t, g):
        keys = kw[pl.ds(t, 5), :, g * DH : (g + 1) * DH].reshape(5 * TOK, DH)
        vals = vw[pl.ds(t, 5), :, g * DH : (g + 1) * DH].reshape(5 * TOK, DH)
        grad = stacked(gobuf, t, g)
        p = pbuf[t * 2 + g]
        out = nn(p, vals).astype(BF16)
        delta = jnp.sum(grad.astype(F32) * out.astype(F32), axis=1, keepdims=True)
        dsbuf[...] = (p.astype(F32) * (nt(grad, vals) - delta)).astype(BF16)
        dk = tn(dsbuf[...], stacked(qbuf, t, g)) * SCALE
        dkw[pl.ds(t, 5), :, g * DH : (g + 1) * DH] += dk.reshape(5, TOK, DH)
        dq = (nn(dsbuf[...], keys) * SCALE).astype(BF16)
        for r in range(4):
            qc = slice(g * 512 + r * DH, g * 512 + (r + 1) * DH)
            obuf[t, :, qc] = out[r * TOK : (r + 1) * TOK]
            dqbuf[t, :, qc] = dq[r * TOK : (r + 1) * TOK]

    for g in range(2):
        now("v%d" % g)
        cols = slice(g * DH, (g + 1) * DH)

        @pl.loop(0, 2)
        def _(t):
            path_b(t, g)

        if g == 0:
            scatter_third()
        for j in range(4):
            dks[g, j] = dkw[j, :, cols].astype(BF16)
        dksib_s[g] = dkw[4 + o, :, cols]
        for k in (1, 2):
            for t in range(2):
                i = g * 4 + (k - 1) * 2
                copy = remote(
                    dks.at[g, (2 - k) * 2 + t], dkr.at[i + c], dk_s.at[i + t], dk_r.at[i + c], chip(-k) * 2 + t
                )
                copy.start()
                later("sent", copy.wait_send)
        go(remote(dksib_s.at[g], dksib.at[g], dk_s.at[8 + g], dk_r.at[8 + g], sibling), "dk")
        for i in range(g * 4, g * 4 + 4):
            later("dk", lambda i=i: arrived(dkr.at[i], dk_s.at[i], dk_r.at[i]))

    for i, (buf, out) in enumerate(((obuf, o_out), (dqbuf, dq_out))):
        go(remote(buf.at[o], out.at[:, own_q], sib_s.at[6 + i], sib_r.at[6 + i], sibling), "none")
        pending[:] = [p for p in pending if p[0] != "none"]
        at = out.at[:, oth_q]
        later("out", lambda i=i, at=at: arrived(at, sib_s.at[6 + i], sib_r.at[6 + i]))
        copy = pltpu.make_async_copy(buf.at[c], out.at[:, own_q], loc.at[8 + i])
        copy.start()
        later("sent", copy.wait)

    now("dk")
    for g in range(2):
        own = dkw[4 + c, :, g * DH : (g + 1) * DH]
        own = own + dkr[g * 4 + c].astype(F32) + dkr[g * 4 + 2 + c].astype(F32)
        oth = dksib[g] + dkr[g * 4 + o].astype(F32) + dkr[g * 4 + 2 + o].astype(F32)
        gk_out[:, pl.ds(aligned(c * HALF + g * DH, DH), DH)] = own.astype(BF16)
        gk_out[:, pl.ds(aligned(o * HALF + g * DH, DH), DH)] = oth.astype(BF16)

    now("rs3")
    acc = r3[0].astype(F32)
    for zz in range(1, NZ):
        acc = acc + r3[zz].astype(F32)
    gx[c] = jnp.concatenate([acc[:8], acc[8:]], 1)
    go(remote(gx.at[c], gx.at[c], sib_s.at[8], sib_r.at[8], sibling), "none")
    pending[:] = [p for p in pending if p[0] != "none"]
    now("adam")
    arrived(gx.at[o], sib_s.at[8], sib_r.at[8])
    both = jnp.concatenate([gx[0], gx[1]], 1)
    grad = jnp.where(c == 0, both[:4], both[4:])
    first = beta_first * adam[1] + (1.0 - beta_first) * grad
    second = beta_second * adam[2] + (1.0 - beta_second) * grad * grad
    nm_out[...] = first
    nv_out[...] = second
    first_hat = first / (1.0 - beta_first**OPT_STEP)
    second_hat = second / (1.0 - beta_second**OPT_STEP)
    w = adam[0]
    nw_out[...] = w - learning * (first_hat / (jnp.sqrt(second_hat) + epsilon) + decay_rate * w)

    for key, wait in pending:
        wait()


def settle(*refs):
    sems = refs[-1]
    copies = [pltpu.make_async_copy(refs[i], refs[7 + i], sems.at[i]) for i in range(7)]
    for copy in copies:
        copy.start()
    for copy in copies:
        copy.wait()


def shards(hidden, queries, key_rows, grad_out, master_value, adam_first, adam_second):
    ZH = NZ // ZL
    ROWS = ZL * 8
    PG = NY * ROWS
    NG = NX * ZH
    V = pltpu.VMEM
    DMA = pltpu.SemaphoreType.DMA
    scratch = [
        V((2, TOK, NG * PG), BF16),
        V((2, TOK, QHALF), BF16),
        V((2, TOK, QHALF), BF16),
        V((6, TOK, HALF), BF16),
        V((6, TOK, HALF), BF16),
        V((2, 4, HALF), F32),
        V((NZ, 16, 128), BF16),
        V((2, NG, NY, ROWS, HALF), BF16),
        V((2, TOK, 5 * TOK), F32),
        V((PG, PG), BF16),
        V((NG, 2 * TOK, PG), BF16),
        V((NG, PG, 2 * TOK), BF16),
        V((4, 4 * TOK, 5 * TOK), BF16),
        V((4 * TOK, 5 * TOK), BF16),
        V((6, TOK, HALF), F32),
        V((6, TOK, HALF), F32),
        V((2, 4, TOK, DH), BF16),
        V((4, 2, TOK, DH), BF16),
        V((2, 4, TOK, DH), BF16),
        V((8, TOK, DH), BF16),
        V((2, TOK, DH), F32),
        V((2, TOK, DH), F32),
        V((2, TOK, HALF), BF16),
        V((2, TOK, HALF), BF16),
        V((NG, NY, ROWS, HALF), BF16),
        V((NX - 1, ZH, NY, ROWS, HALF), BF16),
        V((NY - 1, NG, ROWS, HALF), BF16),
        V((ZH, NY, ROWS, HALF), BF16),
        V((NG, ROWS, HALF), BF16),
        V((NX - 1, ZH, ROWS, HALF), BF16),
        V((ZH, ROWS, HALF), F32),
        V((NZ, 16, 128), BF16),
        V((NZ, 16, 128), BF16),
        V((2, 8, HALF), F32),
        V((2, TOK, QHALF), BF16),
        V((2, TOK, QHALF), BF16),
        V((3, 4, 2 * HALF), F32),
        V((TOK, NG * PG), BF16),
        DMA((11,)),
        DMA((9,)), DMA((9,)),
        DMA((5,)), DMA((6,)),
        DMA((4,)), DMA((4,)),
        DMA((4,)), DMA((4,)),
        DMA((10,)), DMA((10,)),
        DMA((NZ,)), DMA((NZ,)),
        DMA((NX - 1,)), DMA((NX - 1,)),
        DMA((NY * (NX - 1),)), DMA((NY * (NX - 1),)),
        DMA((2 * (NX - 1),)), DMA((2 * (NX - 1),)),
        DMA((NX - 1,)), DMA((NX - 1,)),
        DMA((NZ,)), DMA((NZ,)),
    ]
    hbm = pl.BlockSpec(memory_space=pltpu.HBM)
    anywhere = pl.BlockSpec(memory_space=pl.ANY)
    vmem = pl.BlockSpec(memory_space=pltpu.VMEM)
    outs = (queries, queries, key_rows, hidden, master_value, adam_first, adam_second)
    shapes = tuple(jax.ShapeDtypeStruct(a.shape, a.dtype) for a in outs)
    results = pl.pallas_call(
        kernel,
        out_shape=shapes,
        in_specs=[hbm] * 7,
        out_specs=(anywhere, anywhere, vmem, anywhere, vmem, vmem, vmem),
        scratch_shapes=scratch,
        compiler_params=pltpu.CompilerParams(
            collective_id=0, has_side_effects=True, vmem_limit_bytes=52 * 1024 * 1024
        ),
    )(
        *(
            pltpu.with_memory_space_constraint(a, pltpu.HBM)
            for a in (hidden, queries, key_rows, grad_out, master_value, adam_first, adam_second)
        )
    )
    return pl.pallas_call(
        settle,
        out_shape=shapes,
        in_specs=[anywhere] * 7,
        out_specs=(hbm,) * 7,
        scratch_shapes=[DMA((7,))],
        compiler_params=pltpu.CompilerParams(vmem_limit_bytes=2 * 1024 * 1024),
    )(*results)


def solution(mesh):
    placed = (P("seq", None),) * 7
    return jax.shard_map(
        shards, mesh=mesh, in_specs=placed, out_specs=placed, check_vma=False
    )
```

```python
import math

import jax
import jax.numpy as jnp
from jax import lax
from jax.experimental import pallas as pl
from jax.experimental.pallas import tpu as pltpu
from jax.sharding import PartitionSpec as P

HQ = 16
HK = 4
DH = 128
WINDOW = 512
OPT_STEP = 10
TOK = 128
SCALE = 1.0 / math.sqrt(DH)

beta_first = 0.9
beta_second = 0.95
learning = 0.001
decay_rate = 0.1
epsilon = 1e-08

F32 = jnp.float32
BF16 = jnp.bfloat16
MESH = pl.DeviceIdType.MESH

NX, NZ, NY = 4, 16, 4
ZL = 8
HALF = 256
QHALF = 1024


def nt(a, b):
    return lax.dot_general(a, b, (((1,), (1,)), ((), ())), preferred_element_type=F32)


def nn(a, b):
    return lax.dot_general(a, b, (((1,), (0,)), ((), ())), preferred_element_type=F32)


def tn(a, b):
    return lax.dot_general(a, b, (((0,), (0,)), ((), ())), preferred_element_type=F32)


def aligned(value, multiple):
    return pl.multiple_of(value, multiple)


def kernel(
    hid_ref, q_ref, k_ref, go_ref, w_ref, m_ref, v_ref,
    o_out, dq_out, gk_out, gh_out, nw_out, nm_out, nv_out,
    hbuf, qbuf, gobuf, kw, vw, wsib, wz, w2, bias, perm, hp, ht, pbuf, dsbuf,
    dvw, dkw, dvs, dvr, dks, dkr, dksib, dksib_s, dval, dx,
    gbuf, r1, s1, r2, t2, z3, r3, gx, obuf, dqbuf, adam, ghbuf,
    loc, sib_s, sib_r, k_s, k_r, v_s, v_r, dv_s, dv_r, dk_s, dk_r,
    ag1_s, ag1_r, ag2_s, ag2_r, ag3_s, ag3_r, rs1_s, rs1_r, rs2_s, rs2_r, rs3_s, rs3_r,
):
    ZH = NZ // ZL
    ROWS = ZL * 8
    PG = NY * ROWS
    NG = NX * ZH
    NCHIP = NX * NZ * NY
    d = lax.axis_index("seq")
    c = d % 2
    o = 1 - c
    n = d // 2
    y = n % NY
    z = (n // NY) % NZ
    x = n // (NY * NZ)

    def chip(step):
        return (n + step + NCHIP) % NCHIP

    def dev(x_, z_, y_):
        return ((x_ * NZ + z_) * NY + y_) * 2 + c

    sibling = n * 2 + o

    def remote(src, dst, ssem, rsem, device):
        return pltpu.make_async_remote_copy(
            src_ref=src, dst_ref=dst, send_sem=ssem, recv_sem=rsem,
            device_id=(device,), device_id_type=MESH,
        )

    def x_peer(k):
        return (x + k) % NX

    def y_peer(k):
        return (y + k) % NY

    pending = []

    def later(key, wait):
        pending.append((key, wait))

    def now(key):
        for item in [p for p in pending if p[0] == key]:
            item[1]()
            pending.remove(item)

    def go(copy, key):
        copy.start()
        later(key, copy.wait_recv)
        later("sent", copy.wait_send)

    def arrived(dst, ssem, rsem):
        remote(dst, dst, ssem, rsem, sibling).wait_recv()

    def on_core(which, act):
        @pl.when(c == which)
        def _():
            act()

    def along(key, zero, one):
        for which, (send, wait) in ((0, zero), (1, one)):
            def start(send=send):
                for k in (2, 1, 3) if NX == 4 else range(1, NX):
                    send(k).start()

            def got(wait=wait):
                for k in range(1, NX):
                    wait(k).wait_recv()

            def left(send=send):
                for k in range(1, NX):
                    send(k).wait_send()

            on_core(which, start)
            later(key, lambda which=which, act=got: on_core(which, act))
            later("sent", lambda which=which, act=left: on_core(which, act))

    def ring(key, send, wait):
        @pl.loop(0, NZ - 1)
        def _(i):
            far = (i + 1) // 2
            send(NZ // 2 + jnp.where(i % 2 == 0, far, -far)).start()

        def got():
            @pl.loop(1, NZ)
            def _(k):
                wait(k).wait_recv()

        def left():
            @pl.loop(1, NZ)
            def _(k):
                send(k).wait_send()

        later(key, got)
        later("sent", left)

    barrier = pltpu.get_barrier_semaphore()

    def greet(device):
        pl.semaphore_signal(barrier, inc=1, device_id=(device,), device_id_type=MESH)

    @pl.loop(0, NZ - 1)
    def _(i):
        far = (i + 1) // 2
        greet(dev(x, (z + NZ // 2 + jnp.where(i % 2 == 0, far, -far)) % NZ, y))

    for k in range(1, NX):
        greet(dev(x_peer(k), z, y))
    for k in range(1, NY):
        greet(dev(x, z, y_peer(k)))
    for step in (-2, -1, 1, 2):
        for h in range(2):
            greet(chip(step) * 2 + h)
    greet(sibling)

    own_q = pl.ds(aligned(c * QHALF, QHALF), QHALF)
    oth_q = pl.ds(aligned(o * QHALF, QHALF), QHALF)
    own_k = pl.ds(aligned(c * HALF, HALF), HALF)
    oth_k = pl.ds(aligned(o * HALF, HALF), HALF)

    for i, (key, src, dst) in enumerate(
        (
            ("w", w_ref.at[:, own_k], wsib.at[c]),
            ("k", k_ref.at[:, own_k], kw.at[4 + c]),
            ("q", q_ref.at[:, own_q], qbuf.at[c]),
            ("q", go_ref.at[:, own_q], gobuf.at[c]),
            ("hid", hid_ref, hbuf.at[c]),
            ("adam", w_ref, adam.at[0]),
            ("adam", m_ref, adam.at[1]),
            ("adam", v_ref, adam.at[2]),
        )
    ):
        copy = pltpu.make_async_copy(src, dst, loc.at[i])
        copy.start()
        later(key, copy.wait)

    row = lax.broadcasted_iota(jnp.int32, (TOK, 5 * TOK), 0)
    col = lax.broadcasted_iota(jnp.int32, (TOK, 5 * TOK), 1)
    relative = row + WINDOW - col
    for t in range(2):
        first = (d - c + t) * TOK - WINDOW
        allowed = (relative >= 0) & (relative < WINDOW) & (col + first >= 0)
        bias[t] = jnp.where(allowed, 0.0, -1e30).astype(F32)
    prow = lax.broadcasted_iota(jnp.int32, (PG, PG), 0)
    pcol = lax.broadcasted_iota(jnp.int32, (PG, PG), 1)
    source = ((prow % ROWS) // 8) * (NY * 8) + (prow // ROWS) * 8 + prow % 8
    perm[...] = jnp.where(source == pcol, 1.0, 0.0).astype(BF16)
    dvw[...] = jnp.zeros(dvw.shape, F32)
    dkw[...] = jnp.zeros(dkw.shape, F32)

    pl.semaphore_wait(barrier, 1 + 8 + (NX - 1) + (NY - 1) + (NZ - 1))

    go(remote(w_ref.at[:, oth_k], wsib.at[c], sib_s.at[0], sib_r.at[0], sibling), "w")
    go(remote(k_ref.at[:, oth_k], kw.at[4 + c], k_s.at[0], k_r.at[4 + c], sibling), "none")
    for i, (step, h) in enumerate(((1, 0), (1, 1), (2, 0), (2, 1))):
        slot = (2 - step) * 2 + c
        go(
            remote(
                k_ref.at[:, h * HALF : (h + 1) * HALF], kw.at[slot], k_s.at[1 + i], k_r.at[slot],
                chip(step) * 2 + h,
            ),
            "none",
        )
    pending[:] = [p for p in pending if p[0] != "none"]

    def keys_in():
        arrived(kw.at[4 + o], k_s.at[0], k_r.at[4 + o])
        for slot in (2, 3, 0, 1):
            arrived(kw.at[slot], k_s.at[0], k_r.at[slot])

    later("k", keys_in)
    go(remote(q_ref.at[:, oth_q], qbuf.at[c], sib_s.at[1], sib_r.at[1], sibling), "q")
    go(remote(go_ref.at[:, oth_q], gobuf.at[c], sib_s.at[2], sib_r.at[2], sibling), "q")
    go(remote(hid_ref, hbuf.at[c], sib_s.at[3], sib_r.at[3], sibling), "hid")

    now("w")
    block = jnp.concatenate([wsib[0], wsib[1]], 0)
    wz[z] = jnp.concatenate([block[:, :128], block[:, 128:]], 0).astype(BF16)

    def ag1(k):
        return remote(wz.at[z], wz.at[z], ag1_s.at[k], ag1_r.at[k], dev(x, (z + k) % NZ, y))

    def ag1_in(k):
        slot = (z - k + NZ) % NZ
        return remote(wz.at[slot], wz.at[slot], ag1_s.at[k], ag1_r.at[k], sibling)

    ring("ag1", ag1, ag1_in)

    def ag2_x(k, who):
        at = w2.at[c, pl.ds(who * ZH, ZH), y]
        return remote(at, at, ag2_s.at[k - 1], ag2_r.at[k - 1], dev(x_peer(k), z, y))

    def ag2_y(k, who):
        at = w2.at[c, pl.ds(x * ZH, ZH), who]
        return remote(at, at, ag2_s.at[k - 1], ag2_r.at[k - 1], dev(x, z, y_peer(k)))

    def ag3_x(j, k, who):
        at = w2.at[c, pl.ds(who * ZH, ZH), (y - j + NY) % NY]
        i = j * (NX - 1) + k - 1
        return remote(at, at, ag3_s.at[i], ag3_r.at[i], dev(x_peer(k), z, y))

    def ag3_y(j, k, who):
        at = w2.at[c, pl.ds(((x - j + NX) % NX) * ZH, ZH), who]
        i = j * (NX - 1) + k - 1
        return remote(at, at, ag3_s.at[i], ag3_r.at[i], dev(x, z, y_peer(k)))

    def gather_third(j):
        along(
            "ag3",
            (lambda k: ag3_x(j, k, x), lambda k: ag3_x(j, k, (x - k + NX) % NX)),
            (lambda k: ag3_y(j, k, y), lambda k: ag3_y(j, k, (y - k + NY) % NY)),
        )

    def gather_second():
        now("ag1")
        for zh in range(ZH):
            rows = []
            for zl in range(ZL):
                block = wz[zh * ZL + zl].astype(F32)
                rows.append(jnp.concatenate([block[:8], block[8:]], 1))
            w2[c, x * ZH + zh, y] = jnp.concatenate(rows, 0).astype(BF16)
        along(
            "ag2",
            (lambda k: ag2_y(k, y), lambda k: ag2_y(k, (y - k + NY) % NY)),
            (lambda k: ag2_x(k, x), lambda k: ag2_x(k, (x - k + NX) % NX)),
        )
        gather_third(0)

    def path_a(t, g):
        keys = kw[pl.ds(t, 5), :, g * DH : (g + 1) * DH].reshape(5 * TOK, DH)
        grads = []
        for r in range(4):
            qc = slice(g * 512 + r * DH, g * 512 + (r + 1) * DH)
            s = nt(qbuf[t, :, qc], keys) + bias[t]
            top = jnp.max(s, axis=1, keepdims=True)
            e = jnp.exp2((s - top) * (SCALE * math.log2(math.e)))
            inv = 1.0 / jnp.sum(e, axis=1, keepdims=True)
            pbuf[t * 2 + g, r * TOK : (r + 1) * TOK, :] = (e * inv).astype(BF16)
            grads.append(gobuf[t, :, qc])
        dv = tn(pbuf[t * 2 + g], jnp.concatenate(grads, 0))
        dvw[pl.ds(t, 5), :, g * DH : (g + 1) * DH] += dv.reshape(5, TOK, DH)

    gather_second()
    now("k")
    now("q")
    for g in range(2):
        @pl.loop(0, 2)
        def _(t):
            path_a(t, g)

        for j in range(4):
            dvs[g, j] = dvw[j, :, g * DH : (g + 1) * DH].astype(BF16)
        for k in (1, 2):
            i = g * 2 + k - 1
            go(
                remote(dvs.at[g, pl.ds((2 - k) * 2, 2)], dvr.at[i], dv_s.at[i], dv_r.at[i], chip(-k) * 2 + c),
                "dv%d" % g,
            )

    now("ag2")
    for j in range(1, NY):
        gather_third(j)

    now("hid")

    @pl.loop(0, NG)
    def _(g):
        cols = pl.ds(aligned(g * PG, PG), PG)
        both = jnp.concatenate([hbuf[0, :, cols], hbuf[1, :, cols]], 0)
        hp[g] = nt(both, perm[...]).astype(BF16)
        ht[g] = nt(perm[...], both).astype(BF16)

    def spot(k, j):
        x_ = (x + jnp.where(c == 0, k, j)) % NX
        y_ = (y + jnp.where(c == 0, j, k)) % NY
        return x_, y_

    def slab(k, j):
        x_, y_ = spot(k, j)
        return pl.ds(x_ * ZH, ZH), y_

    def rs1(k, j):
        x_, y_ = spot(k, 0)
        i = j * (NX - 1) + k - 1
        return remote(gbuf.at[slab(k, j)], r1.at[k - 1, j], rs1_s.at[i], rs1_r.at[i], dev(x_, z, y_))

    def rs2(j):
        x_, y_ = spot(0, j)
        return remote(s1.at[j - 1], r2.at[j - 1], rs2_s.at[j - 1], rs2_r.at[j - 1], dev(x_, z, y_))

    far = (2, 1, 3) if NX == 4 else tuple(range(1, NX))
    for g in range(2):
        now("dv%d" % g)
        low = slice(g * DH, (g + 1) * DH)
        total = dvw[4:6, :, low] + dvr[g * 2].astype(F32) + dvr[g * 2 + 1].astype(F32)
        dval[:, :, low] = total.astype(BF16)

    @pl.loop(0, NG)
    def _(f):
        gw = nn(ht[f], dval[...].reshape(2 * TOK, HALF))
        gbuf[f] = gw.astype(BF16).reshape(NY, ROWS, HALF)

    for j in far + (0,):
        for k in far:
            go(rs1(k, j), "rs1_%d" % j)

    dx[c] = dval[c]
    go(remote(dval.at[o], dx.at[c], sib_s.at[5], sib_r.at[5], sibling), "dx")

    now("ag3")
    values = jnp.zeros((2 * TOK, HALF), F32)
    for g in range(NG):
        values = values + nn(hp[g], w2[c, g].reshape(PG, HALF))
    values = values.astype(BF16)
    vw[4] = values[:TOK]
    vw[5] = values[TOK:]
    for g in range(2):
        low = slice(g * DH, (g + 1) * DH)
        for k in (1, 2):
            i = g * 2 + k - 1
            at = vw.at[pl.ds((2 - k) * 2, 2), :, low]
            copy = remote(vw.at[4:6, :, low], at, v_s.at[i], v_r.at[i], chip(k) * 2 + c)
            copy.start()
            later("sent", copy.wait_send)
            later("v%d" % g, lambda at=at, i=i: arrived(at, v_s.at[i], v_r.at[i]))
    go(remote(w2.at[c], w2.at[c], sib_s.at[4], sib_r.at[4], sibling), "none")
    pending[:] = [p for p in pending if p[0] != "none"]
    later("w2", lambda: arrived(w2.at[o], sib_s.at[4], sib_r.at[4]))

    now("dx")
    now("w2")

    @pl.loop(0, NG)
    def _(g):
        both = nt(dx[0], w2[0, g].reshape(PG, HALF)) + nt(dx[1], w2[1, g].reshape(PG, HALF))
        ghbuf[:, pl.ds(aligned(g * PG, PG), PG)] = nn(both.astype(BF16), perm[...]).astype(BF16)

    copy = pltpu.make_async_copy(ghbuf, gh_out, loc.at[10])
    copy.start()
    later("sent", copy.wait)

    for j in far + (0,):
        now("rs1_%d" % j)
        part = gbuf[slab(0, j)].astype(F32)
        for k in range(1, NX):
            part = part + r1[k - 1, j].astype(F32)
        if j == 0:
            t2[...] = part
        else:
            s1[j - 1] = part.astype(BF16)
            go(rs2(j), "rs2")

    def rs3(k):
        z_ = (z + k) % NZ
        return remote(z3.at[z_], r3.at[z], rs3_s.at[k], rs3_r.at[k], dev(x, z_, y))

    def rs3_in(k):
        slot = (z - k + NZ) % NZ
        return remote(r3.at[slot], r3.at[slot], rs3_s.at[k], rs3_r.at[k], sibling)

    def scatter_third():
        now("rs2")
        part = t2[...]
        for k in range(1, NX):
            part = part + r2[k - 1].astype(F32)
        part = part.reshape(NZ, 8, HALF)
        for zz in range(NZ):
            z3[zz] = jnp.concatenate([part[zz, :, :128], part[zz, :, 128:]], 0).astype(BF16)
        ring("rs3", rs3, rs3_in)
        r3[z] = z3[z]

    def stacked(ref, t, g):
        return jnp.concatenate([ref[t, :, g * 512 + r * DH : g * 512 + (r + 1) * DH] for r in range(4)], 0)

    def path_b(t, g):
        keys = kw[pl.ds(t, 5), :, g * DH : (g + 1) * DH].reshape(5 * TOK, DH)
        vals = vw[pl.ds(t, 5), :, g * DH : (g + 1) * DH].reshape(5 * TOK, DH)
        grad = stacked(gobuf, t, g)
        p = pbuf[t * 2 + g]
        out = nn(p, vals).astype(BF16)
        delta = jnp.sum(grad.astype(F32) * out.astype(F32), axis=1, keepdims=True)
        dsbuf[...] = (p.astype(F32) * (nt(grad, vals) - delta)).astype(BF16)
        dk = tn(dsbuf[...], stacked(qbuf, t, g)) * SCALE
        dkw[pl.ds(t, 5), :, g * DH : (g + 1) * DH] += dk.reshape(5, TOK, DH)
        dq = (nn(dsbuf[...], keys) * SCALE).astype(BF16)
        for r in range(4):
            qc = slice(g * 512 + r * DH, g * 512 + (r + 1) * DH)
            obuf[t, :, qc] = out[r * TOK : (r + 1) * TOK]
            dqbuf[t, :, qc] = dq[r * TOK : (r + 1) * TOK]

    for g in range(2):
        now("v%d" % g)
        cols = slice(g * DH, (g + 1) * DH)

        @pl.loop(0, 2)
        def _(t):
            path_b(t, g)

        if g == 0:
            scatter_third()
        for j in range(4):
            dks[g, j] = dkw[j, :, cols].astype(BF16)
        dksib_s[g] = dkw[4 + o, :, cols]
        for k in (1, 2):
            for t in range(2):
                i = g * 4 + (k - 1) * 2
                copy = remote(
                    dks.at[g, (2 - k) * 2 + t], dkr.at[i + c], dk_s.at[i + t], dk_r.at[i + c], chip(-k) * 2 + t
                )
                copy.start()
                later("sent", copy.wait_send)
        go(remote(dksib_s.at[g], dksib.at[g], dk_s.at[8 + g], dk_r.at[8 + g], sibling), "dk")
        for i in range(g * 4, g * 4 + 4):
            later("dk", lambda i=i: arrived(dkr.at[i], dk_s.at[i], dk_r.at[i]))

    for i, (buf, out) in enumerate(((obuf, o_out), (dqbuf, dq_out))):
        go(remote(buf.at[o], out.at[:, own_q], sib_s.at[6 + i], sib_r.at[6 + i], sibling), "none")
        pending[:] = [p for p in pending if p[0] != "none"]
        at = out.at[:, oth_q]
        later("out", lambda i=i, at=at: arrived(at, sib_s.at[6 + i], sib_r.at[6 + i]))
        copy = pltpu.make_async_copy(buf.at[c], out.at[:, own_q], loc.at[8 + i])
        copy.start()
        later("sent", copy.wait)

    now("dk")
    for g in range(2):
        own = dkw[4 + c, :, g * DH : (g + 1) * DH]
        own = own + dkr[g * 4 + c].astype(F32) + dkr[g * 4 + 2 + c].astype(F32)
        oth = dksib[g] + dkr[g * 4 + o].astype(F32) + dkr[g * 4 + 2 + o].astype(F32)
        gk_out[:, pl.ds(aligned(c * HALF + g * DH, DH), DH)] = own.astype(BF16)
        gk_out[:, pl.ds(aligned(o * HALF + g * DH, DH), DH)] = oth.astype(BF16)

    now("rs3")
    acc = r3[0].astype(F32)
    for zz in range(1, NZ):
        acc = acc + r3[zz].astype(F32)
    gx[c] = jnp.concatenate([acc[:8], acc[8:]], 1)
    go(remote(gx.at[c], gx.at[c], sib_s.at[8], sib_r.at[8], sibling), "none")
    pending[:] = [p for p in pending if p[0] != "none"]
    now("adam")
    arrived(gx.at[o], sib_s.at[8], sib_r.at[8])
    both = jnp.concatenate([gx[0], gx[1]], 1)
    grad = jnp.where(c == 0, both[:4], both[4:])
    first = beta_first * adam[1] + (1.0 - beta_first) * grad
    second = beta_second * adam[2] + (1.0 - beta_second) * grad * grad
    nm_out[...] = first
    nv_out[...] = second
    first_hat = first / (1.0 - beta_first**OPT_STEP)
    second_hat = second / (1.0 - beta_second**OPT_STEP)
    w = adam[0]
    nw_out[...] = w - learning * (first_hat / (jnp.sqrt(second_hat) + epsilon) + decay_rate * w)

    for key, wait in pending:
        wait()


def settle(*refs):
    sems = refs[-1]
    copies = [pltpu.make_async_copy(refs[i], refs[7 + i], sems.at[i]) for i in range(7)]
    for copy in copies:
        copy.start()
    for copy in copies:
        copy.wait()


def shards(hidden, queries, key_rows, grad_out, master_value, adam_first, adam_second):
    ZH = NZ // ZL
    ROWS = ZL * 8
    PG = NY * ROWS
    NG = NX * ZH
    V = pltpu.VMEM
    DMA = pltpu.SemaphoreType.DMA
    scratch = [
        V((2, TOK, NG * PG), BF16),
        V((2, TOK, QHALF), BF16),
        V((2, TOK, QHALF), BF16),
        V((6, TOK, HALF), BF16),
        V((6, TOK, HALF), BF16),
        V((2, 4, HALF), F32),
        V((NZ, 16, 128), BF16),
        V((2, NG, NY, ROWS, HALF), BF16),
        V((2, TOK, 5 * TOK), F32),
        V((PG, PG), BF16),
        V((NG, 2 * TOK, PG), BF16),
        V((NG, PG, 2 * TOK), BF16),
        V((4, 4 * TOK, 5 * TOK), BF16),
        V((4 * TOK, 5 * TOK), BF16),
        V((6, TOK, HALF), F32),
        V((6, TOK, HALF), F32),
        V((2, 4, TOK, DH), BF16),
        V((4, 2, TOK, DH), BF16),
        V((2, 4, TOK, DH), BF16),
        V((8, TOK, DH), BF16),
        V((2, TOK, DH), F32),
        V((2, TOK, DH), F32),
        V((2, TOK, HALF), BF16),
        V((2, TOK, HALF), BF16),
        V((NG, NY, ROWS, HALF), BF16),
        V((NX - 1, NY, ZH, ROWS, HALF), BF16),
        V((NY - 1, ZH, ROWS, HALF), BF16),
        V((NX - 1, ZH, ROWS, HALF), BF16),
        V((ZH, ROWS, HALF), F32),
        V((NZ, 16, 128), BF16),
        V((NZ, 16, 128), BF16),
        V((2, 8, HALF), F32),
        V((2, TOK, QHALF), BF16),
        V((2, TOK, QHALF), BF16),
        V((3, 4, 2 * HALF), F32),
        V((TOK, NG * PG), BF16),
        DMA((11,)),
        DMA((9,)), DMA((9,)),
        DMA((5,)), DMA((6,)),
        DMA((4,)), DMA((4,)),
        DMA((4,)), DMA((4,)),
        DMA((10,)), DMA((10,)),
        DMA((NZ,)), DMA((NZ,)),
        DMA((NX - 1,)), DMA((NX - 1,)),
        DMA((NY * (NX - 1),)), DMA((NY * (NX - 1),)),
        DMA((NY * (NX - 1),)), DMA((NY * (NX - 1),)),
        DMA((NX - 1,)), DMA((NX - 1,)),
        DMA((NZ,)), DMA((NZ,)),
    ]
    hbm = pl.BlockSpec(memory_space=pltpu.HBM)
    anywhere = pl.BlockSpec(memory_space=pl.ANY)
    vmem = pl.BlockSpec(memory_space=pltpu.VMEM)
    outs = (queries, queries, key_rows, hidden, master_value, adam_first, adam_second)
    shapes = tuple(jax.ShapeDtypeStruct(a.shape, a.dtype) for a in outs)
    results = pl.pallas_call(
        kernel,
        out_shape=shapes,
        in_specs=[hbm] * 7,
        out_specs=(anywhere, anywhere, vmem, anywhere, vmem, vmem, vmem),
        scratch_shapes=scratch,
        compiler_params=pltpu.CompilerParams(
            collective_id=0, has_side_effects=True, vmem_limit_bytes=52 * 1024 * 1024
        ),
    )(
        *(
            pltpu.with_memory_space_constraint(a, pltpu.HBM)
            for a in (hidden, queries, key_rows, grad_out, master_value, adam_first, adam_second)
        )
    )
    return pl.pallas_call(
        settle,
        out_shape=shapes,
        in_specs=[anywhere] * 7,
        out_specs=(hbm,) * 7,
        scratch_shapes=[DMA((7,))],
        compiler_params=pltpu.CompilerParams(vmem_limit_bytes=2 * 1024 * 1024),
    )(*results)


def solution(mesh):
    placed = (P("seq", None),) * 7
    return jax.shard_map(
        shards, mesh=mesh, in_specs=placed, out_specs=placed, check_vma=False
    )
```

```python
import math

import jax
import jax.numpy as jnp
from jax import lax
from jax.experimental import pallas as pl
from jax.experimental.pallas import tpu as pltpu
from jax.sharding import PartitionSpec as P

HQ = 16
HK = 4
DH = 128
WINDOW = 512
OPT_STEP = 10
TOK = 128
SCALE = 1.0 / math.sqrt(DH)

beta_first = 0.9
beta_second = 0.95
learning = 0.001
decay_rate = 0.1
epsilon = 1e-08

F32 = jnp.float32
BF16 = jnp.bfloat16
MESH = pl.DeviceIdType.MESH

NX, NZ, NY = 4, 16, 4
ZL = 8
HALF = 256
QHALF = 1024


def nt(a, b):
    return lax.dot_general(a, b, (((1,), (1,)), ((), ())), preferred_element_type=F32)


def nn(a, b):
    return lax.dot_general(a, b, (((1,), (0,)), ((), ())), preferred_element_type=F32)


def tn(a, b):
    return lax.dot_general(a, b, (((0,), (0,)), ((), ())), preferred_element_type=F32)


def aligned(value, multiple):
    return pl.multiple_of(value, multiple)


def kernel(
    hid_ref, q_ref, k_ref, go_ref, w_ref, m_ref, v_ref,
    o_out, dq_out, gk_out, gh_out, nw_out, nm_out, nv_out,
    hbuf, qbuf, gobuf, kw, vw, wsib, wz, w2, bias, perm, hp, ht, pbuf, dsbuf,
    dvw, dkw, dvs, dvr, dks, dkr, dksib, dksib_s, dval, dx,
    gbuf, r1, s1, r2, t2, z3, r3, gx, obuf, dqbuf, adam, ghbuf,
    loc, sib_s, sib_r, k_s, k_r, v_s, v_r, dv_s, dv_r, dk_s, dk_r,
    ag1_s, ag1_r, ag2_s, ag2_r, ag3_s, ag3_r, rs1_s, rs1_r, rs2_s, rs2_r, rs3_s, rs3_r,
):
    ZH = NZ // ZL
    ROWS = ZL * 8
    PG = NY * ROWS
    NG = NX * ZH
    NCHIP = NX * NZ * NY
    d = lax.axis_index("seq")
    c = d % 2
    o = 1 - c
    n = d // 2
    y = n % NY
    z = (n // NY) % NZ
    x = n // (NY * NZ)

    def chip(step):
        return (n + step + NCHIP) % NCHIP

    def dev(x_, z_, y_):
        return ((x_ * NZ + z_) * NY + y_) * 2 + c

    sibling = n * 2 + o

    def remote(src, dst, ssem, rsem, device):
        return pltpu.make_async_remote_copy(
            src_ref=src, dst_ref=dst, send_sem=ssem, recv_sem=rsem,
            device_id=(device,), device_id_type=MESH,
        )

    def x_peer(k):
        return (x + k) % NX

    def y_peer(k):
        return (y + k) % NY

    pending = []

    def later(key, wait):
        pending.append((key, wait))

    def now(key):
        for item in [p for p in pending if p[0] == key]:
            item[1]()
            pending.remove(item)

    def go(copy, key):
        copy.start()
        later(key, copy.wait_recv)
        later("sent", copy.wait_send)

    def arrived(dst, ssem, rsem):
        remote(dst, dst, ssem, rsem, sibling).wait_recv()

    def on_core(which, act):
        @pl.when(c == which)
        def _():
            act()

    def along(key, zero, one):
        for which, (send, wait) in ((0, zero), (1, one)):
            def start(send=send):
                for k in (2, 1, 3) if NX == 4 else range(1, NX):
                    send(k).start()

            def got(wait=wait):
                for k in range(1, NX):
                    wait(k).wait_recv()

            def left(send=send):
                for k in range(1, NX):
                    send(k).wait_send()

            on_core(which, start)
            later(key, lambda which=which, act=got: on_core(which, act))
            later("sent", lambda which=which, act=left: on_core(which, act))

    def ring(key, send, wait):
        @pl.loop(0, NZ - 1)
        def _(i):
            far = (i + 1) // 2
            send(NZ // 2 + jnp.where(i % 2 == 0, far, -far)).start()

        def got():
            @pl.loop(1, NZ)
            def _(k):
                wait(k).wait_recv()

        def left():
            @pl.loop(1, NZ)
            def _(k):
                send(k).wait_send()

        later(key, got)
        later("sent", left)

    barrier = pltpu.get_barrier_semaphore()

    def greet(device):
        pl.semaphore_signal(barrier, inc=1, device_id=(device,), device_id_type=MESH)

    @pl.loop(0, NZ - 1)
    def _(i):
        far = (i + 1) // 2
        greet(dev(x, (z + NZ // 2 + jnp.where(i % 2 == 0, far, -far)) % NZ, y))

    for k in range(1, NX):
        greet(dev(x_peer(k), z, y))
    for k in range(1, NY):
        greet(dev(x, z, y_peer(k)))
    for step in (-2, -1, 1, 2):
        for h in range(2):
            greet(chip(step) * 2 + h)
    greet(sibling)

    own_q = pl.ds(aligned(c * QHALF, QHALF), QHALF)
    oth_q = pl.ds(aligned(o * QHALF, QHALF), QHALF)
    own_k = pl.ds(aligned(c * HALF, HALF), HALF)
    oth_k = pl.ds(aligned(o * HALF, HALF), HALF)

    for i, (key, src, dst) in enumerate(
        (
            ("w", w_ref.at[:, own_k], wsib.at[c]),
            ("k", k_ref.at[:, own_k], kw.at[4 + c]),
            ("q", q_ref.at[:, own_q], qbuf.at[c]),
            ("q", go_ref.at[:, own_q], gobuf.at[c]),
            ("hid", hid_ref, hbuf.at[c]),
            ("adam", w_ref, adam.at[0]),
            ("adam", m_ref, adam.at[1]),
            ("adam", v_ref, adam.at[2]),
        )
    ):
        copy = pltpu.make_async_copy(src, dst, loc.at[i])
        copy.start()
        later(key, copy.wait)

    row = lax.broadcasted_iota(jnp.int32, (TOK, 5 * TOK), 0)
    col = lax.broadcasted_iota(jnp.int32, (TOK, 5 * TOK), 1)
    relative = row + WINDOW - col
    for t in range(2):
        first = (d - c + t) * TOK - WINDOW
        allowed = (relative >= 0) & (relative < WINDOW) & (col + first >= 0)
        bias[t] = jnp.where(allowed, 0.0, -1e30).astype(F32)
    prow = lax.broadcasted_iota(jnp.int32, (PG, PG), 0)
    pcol = lax.broadcasted_iota(jnp.int32, (PG, PG), 1)
    source = ((prow % ROWS) // 8) * (NY * 8) + (prow // ROWS) * 8 + prow % 8
    perm[...] = jnp.where(source == pcol, 1.0, 0.0).astype(BF16)
    dvw[...] = jnp.zeros(dvw.shape, F32)
    dkw[...] = jnp.zeros(dkw.shape, F32)

    pl.semaphore_wait(barrier, 1 + 8 + (NX - 1) + (NY - 1) + (NZ - 1))

    go(remote(w_ref.at[:, oth_k], wsib.at[c], sib_s.at[0], sib_r.at[0], sibling), "w")
    go(remote(k_ref.at[:, oth_k], kw.at[4 + c], k_s.at[0], k_r.at[4 + c], sibling), "none")
    for i, (step, h) in enumerate(((1, 0), (1, 1), (2, 0), (2, 1))):
        slot = (2 - step) * 2 + c
        go(
            remote(
                k_ref.at[:, h * HALF : (h + 1) * HALF], kw.at[slot], k_s.at[1 + i], k_r.at[slot],
                chip(step) * 2 + h,
            ),
            "none",
        )
    pending[:] = [p for p in pending if p[0] != "none"]

    def keys_in():
        arrived(kw.at[4 + o], k_s.at[0], k_r.at[4 + o])
        for slot in (2, 3, 0, 1):
            arrived(kw.at[slot], k_s.at[0], k_r.at[slot])

    later("k", keys_in)
    go(remote(q_ref.at[:, oth_q], qbuf.at[c], sib_s.at[1], sib_r.at[1], sibling), "q")
    go(remote(go_ref.at[:, oth_q], gobuf.at[c], sib_s.at[2], sib_r.at[2], sibling), "q")
    go(remote(hid_ref, hbuf.at[c], sib_s.at[3], sib_r.at[3], sibling), "hid")

    now("w")
    block = jnp.concatenate([wsib[0], wsib[1]], 0)
    wz[z] = jnp.concatenate([block[:, :128], block[:, 128:]], 0).astype(BF16)

    def ag1(k):
        return remote(wz.at[z], wz.at[z], ag1_s.at[k], ag1_r.at[k], dev(x, (z + k) % NZ, y))

    def ag1_in(k):
        slot = (z - k + NZ) % NZ
        return remote(wz.at[slot], wz.at[slot], ag1_s.at[k], ag1_r.at[k], sibling)

    ring("ag1", ag1, ag1_in)

    def ag2_x(k, who):
        at = w2.at[c, pl.ds(who * ZH, ZH), y]
        return remote(at, at, ag2_s.at[k - 1], ag2_r.at[k - 1], dev(x_peer(k), z, y))

    def ag2_y(k, who):
        at = w2.at[c, pl.ds(x * ZH, ZH), who]
        return remote(at, at, ag2_s.at[k - 1], ag2_r.at[k - 1], dev(x, z, y_peer(k)))

    def ag3_x(j, k, who):
        at = w2.at[c, pl.ds(who * ZH, ZH), (y - j + NY) % NY]
        i = j * (NX - 1) + k - 1
        return remote(at, at, ag3_s.at[i], ag3_r.at[i], dev(x_peer(k), z, y))

    def ag3_y(j, k, who):
        at = w2.at[c, pl.ds(((x - j + NX) % NX) * ZH, ZH), who]
        i = j * (NX - 1) + k - 1
        return remote(at, at, ag3_s.at[i], ag3_r.at[i], dev(x, z, y_peer(k)))

    def gather_third(j):
        along(
            "ag3",
            (lambda k: ag3_x(j, k, x), lambda k: ag3_x(j, k, (x - k + NX) % NX)),
            (lambda k: ag3_y(j, k, y), lambda k: ag3_y(j, k, (y - k + NY) % NY)),
        )

    def gather_second():
        now("ag1")
        for zh in range(ZH):
            rows = []
            for zl in range(ZL):
                block = wz[zh * ZL + zl].astype(F32)
                rows.append(jnp.concatenate([block[:8], block[8:]], 1))
            w2[c, x * ZH + zh, y] = jnp.concatenate(rows, 0).astype(BF16)
        along(
            "ag2",
            (lambda k: ag2_y(k, y), lambda k: ag2_y(k, (y - k + NY) % NY)),
            (lambda k: ag2_x(k, x), lambda k: ag2_x(k, (x - k + NX) % NX)),
        )
        gather_third(0)

    def path_a(t, g):
        keys = kw[pl.ds(t, 5), :, g * DH : (g + 1) * DH].reshape(5 * TOK, DH)
        grads = []
        for r in range(4):
            qc = slice(g * 512 + r * DH, g * 512 + (r + 1) * DH)
            s = nt(qbuf[t, :, qc], keys) + bias[t]
            top = jnp.max(s, axis=1, keepdims=True)
            e = jnp.exp2((s - top) * (SCALE * math.log2(math.e)))
            inv = 1.0 / jnp.sum(e, axis=1, keepdims=True)
            pbuf[t * 2 + g, r * TOK : (r + 1) * TOK, :] = (e * inv).astype(BF16)
            grads.append(gobuf[t, :, qc])
        dv = tn(pbuf[t * 2 + g], jnp.concatenate(grads, 0))
        dvw[pl.ds(t, 5), :, g * DH : (g + 1) * DH] += dv.reshape(5, TOK, DH)

    gather_second()
    now("k")
    now("q")
    for g in range(2):
        @pl.loop(0, 2)
        def _(t):
            path_a(t, g)

        for j in range(4):
            dvs[g, j] = dvw[j, :, g * DH : (g + 1) * DH].astype(BF16)
        for k in (1, 2):
            i = g * 2 + k - 1
            go(
                remote(dvs.at[g, pl.ds((2 - k) * 2, 2)], dvr.at[i], dv_s.at[i], dv_r.at[i], chip(-k) * 2 + c),
                "dv%d" % g,
            )

    now("ag2")
    for j in range(1, NY):
        gather_third(j)

    now("hid")

    @pl.loop(0, NG)
    def _(g):
        cols = pl.ds(aligned(g * PG, PG), PG)
        both = jnp.concatenate([hbuf[0, :, cols], hbuf[1, :, cols]], 0)
        hp[g] = nt(both, perm[...]).astype(BF16)
        ht[g] = nt(perm[...], both).astype(BF16)

    def spot(k, j):
        x_ = (x + jnp.where(c == 0, k, j)) % NX
        y_ = (y + jnp.where(c == 0, j, k)) % NY
        return x_, y_

    def slab(k, j):
        x_, y_ = spot(k, j)
        return pl.ds(x_ * ZH, ZH), y_

    def rs1(k, j):
        x_, y_ = spot(k, 0)
        i = j * (NX - 1) + k - 1
        return remote(gbuf.at[slab(k, j)], r1.at[k - 1, j], rs1_s.at[i], rs1_r.at[i], dev(x_, z, y_))

    def rs2(j):
        x_, y_ = spot(0, j)
        return remote(s1.at[j - 1], r2.at[j - 1], rs2_s.at[j - 1], rs2_r.at[j - 1], dev(x_, z, y_))

    far = (2, 1, 3) if NX == 4 else tuple(range(1, NX))
    for g in range(2):
        now("dv%d" % g)
        low = slice(g * DH, (g + 1) * DH)
        total = dvw[4:6, :, low] + dvr[g * 2].astype(F32) + dvr[g * 2 + 1].astype(F32)
        dval[:, :, low] = total.astype(BF16)

        @pl.loop(0, NG)
        def _(f):
            gw = nn(ht[f], dval[:, :, low].reshape(2 * TOK, DH))
            gbuf[f, :, :, low] = gw.astype(BF16).reshape(NY, ROWS, DH)

    for j in far + (0,):
        for k in far:
            go(rs1(k, j), "rs1_%d" % j)

    dx[c] = dval[c]
    go(remote(dval.at[o], dx.at[c], sib_s.at[5], sib_r.at[5], sibling), "dx")

    now("ag3")
    values = jnp.zeros((2 * TOK, HALF), F32)
    for g in range(NG):
        values = values + nn(hp[g], w2[c, g].reshape(PG, HALF))
    values = values.astype(BF16)
    vw[4] = values[:TOK]
    vw[5] = values[TOK:]
    for g in range(2):
        low = slice(g * DH, (g + 1) * DH)
        for k in (1, 2):
            i = g * 2 + k - 1
            at = vw.at[pl.ds((2 - k) * 2, 2), :, low]
            copy = remote(vw.at[4:6, :, low], at, v_s.at[i], v_r.at[i], chip(k) * 2 + c)
            copy.start()
            later("sent", copy.wait_send)
            later("v%d" % g, lambda at=at, i=i: arrived(at, v_s.at[i], v_r.at[i]))
    go(remote(w2.at[c], w2.at[c], sib_s.at[4], sib_r.at[4], sibling), "none")
    pending[:] = [p for p in pending if p[0] != "none"]
    later("w2", lambda: arrived(w2.at[o], sib_s.at[4], sib_r.at[4]))

    now("dx")
    now("w2")

    @pl.loop(0, NG)
    def _(g):
        both = nt(dx[0], w2[0, g].reshape(PG, HALF)) + nt(dx[1], w2[1, g].reshape(PG, HALF))
        ghbuf[:, pl.ds(aligned(g * PG, PG), PG)] = nn(both.astype(BF16), perm[...]).astype(BF16)

    copy = pltpu.make_async_copy(ghbuf, gh_out, loc.at[10])
    copy.start()
    later("sent", copy.wait)

    for j in far + (0,):
        now("rs1_%d" % j)
        part = gbuf[slab(0, j)].astype(F32)
        for k in range(1, NX):
            part = part + r1[k - 1, j].astype(F32)
        if j == 0:
            t2[...] = part
        else:
            s1[j - 1] = part.astype(BF16)
            go(rs2(j), "rs2")

    def rs3(k):
        z_ = (z + k) % NZ
        return remote(z3.at[z_], r3.at[z], rs3_s.at[k], rs3_r.at[k], dev(x, z_, y))

    def rs3_in(k):
        slot = (z - k + NZ) % NZ
        return remote(r3.at[slot], r3.at[slot], rs3_s.at[k], rs3_r.at[k], sibling)

    def scatter_third():
        now("rs2")
        part = t2[...]
        for k in range(1, NX):
            part = part + r2[k - 1].astype(F32)
        part = part.reshape(NZ, 8, HALF)
        for zz in range(NZ):
            z3[zz] = jnp.concatenate([part[zz, :, :128], part[zz, :, 128:]], 0).astype(BF16)
        ring("rs3", rs3, rs3_in)
        r3[z] = z3[z]

    def stacked(ref, t, g):
        return jnp.concatenate([ref[t, :, g * 512 + r * DH : g * 512 + (r + 1) * DH] for r in range(4)], 0)

    def path_b(t, g):
        keys = kw[pl.ds(t, 5), :, g * DH : (g + 1) * DH].reshape(5 * TOK, DH)
        vals = vw[pl.ds(t, 5), :, g * DH : (g + 1) * DH].reshape(5 * TOK, DH)
        grad = stacked(gobuf, t, g)
        p = pbuf[t * 2 + g]
        out = nn(p, vals).astype(BF16)
        delta = jnp.sum(grad.astype(F32) * out.astype(F32), axis=1, keepdims=True)
        dsbuf[...] = (p.astype(F32) * (nt(grad, vals) - delta)).astype(BF16)
        dk = tn(dsbuf[...], stacked(qbuf, t, g)) * SCALE
        dkw[pl.ds(t, 5), :, g * DH : (g + 1) * DH] += dk.reshape(5, TOK, DH)
        dq = (nn(dsbuf[...], keys) * SCALE).astype(BF16)
        for r in range(4):
            qc = slice(g * 512 + r * DH, g * 512 + (r + 1) * DH)
            obuf[t, :, qc] = out[r * TOK : (r + 1) * TOK]
            dqbuf[t, :, qc] = dq[r * TOK : (r + 1) * TOK]

    for g in range(2):
        now("v%d" % g)
        cols = slice(g * DH, (g + 1) * DH)

        @pl.loop(0, 2)
        def _(t):
            path_b(t, g)

        if g == 0:
            scatter_third()
        for j in range(4):
            dks[g, j] = dkw[j, :, cols].astype(BF16)
        dksib_s[g] = dkw[4 + o, :, cols]
        for k in (1, 2):
            for t in range(2):
                i = g * 4 + (k - 1) * 2
                copy = remote(
                    dks.at[g, (2 - k) * 2 + t], dkr.at[i + c], dk_s.at[i + t], dk_r.at[i + c], chip(-k) * 2 + t
                )
                copy.start()
                later("sent", copy.wait_send)
        go(remote(dksib_s.at[g], dksib.at[g], dk_s.at[8 + g], dk_r.at[8 + g], sibling), "dk")
        for i in range(g * 4, g * 4 + 4):
            later("dk", lambda i=i: arrived(dkr.at[i], dk_s.at[i], dk_r.at[i]))

    for i, (buf, out) in enumerate(((obuf, o_out), (dqbuf, dq_out))):
        go(remote(buf.at[o], out.at[:, own_q], sib_s.at[6 + i], sib_r.at[6 + i], sibling), "none")
        pending[:] = [p for p in pending if p[0] != "none"]
        at = out.at[:, oth_q]
        later("out", lambda i=i, at=at: arrived(at, sib_s.at[6 + i], sib_r.at[6 + i]))
        copy = pltpu.make_async_copy(buf.at[c], out.at[:, own_q], loc.at[8 + i])
        copy.start()
        later("sent", copy.wait)

    now("dk")
    for g in range(2):
        own = dkw[4 + c, :, g * DH : (g + 1) * DH]
        own = own + dkr[g * 4 + c].astype(F32) + dkr[g * 4 + 2 + c].astype(F32)
        oth = dksib[g] + dkr[g * 4 + o].astype(F32) + dkr[g * 4 + 2 + o].astype(F32)
        gk_out[:, pl.ds(aligned(c * HALF + g * DH, DH), DH)] = own.astype(BF16)
        gk_out[:, pl.ds(aligned(o * HALF + g * DH, DH), DH)] = oth.astype(BF16)

    now("rs3")
    acc = r3[0].astype(F32)
    for zz in range(1, NZ):
        acc = acc + r3[zz].astype(F32)
    gx[c] = jnp.concatenate([acc[:8], acc[8:]], 1)
    go(remote(gx.at[c], gx.at[c], sib_s.at[8], sib_r.at[8], sibling), "none")
    pending[:] = [p for p in pending if p[0] != "none"]
    now("adam")
    arrived(gx.at[o], sib_s.at[8], sib_r.at[8])
    both = jnp.concatenate([gx[0], gx[1]], 1)
    grad = jnp.where(c == 0, both[:4], both[4:])
    first = beta_first * adam[1] + (1.0 - beta_first) * grad
    second = beta_second * adam[2] + (1.0 - beta_second) * grad * grad
    nm_out[...] = first
    nv_out[...] = second
    first_hat = first / (1.0 - beta_first**OPT_STEP)
    second_hat = second / (1.0 - beta_second**OPT_STEP)
    w = adam[0]
    nw_out[...] = w - learning * (first_hat / (jnp.sqrt(second_hat) + epsilon) + decay_rate * w)

    for key, wait in pending:
        wait()


def settle(*refs):
    sems = refs[-1]
    copies = [pltpu.make_async_copy(refs[i], refs[7 + i], sems.at[i]) for i in range(7)]
    for copy in copies:
        copy.start()
    for copy in copies:
        copy.wait()


def shards(hidden, queries, key_rows, grad_out, master_value, adam_first, adam_second):
    ZH = NZ // ZL
    ROWS = ZL * 8
    PG = NY * ROWS
    NG = NX * ZH
    V = pltpu.VMEM
    DMA = pltpu.SemaphoreType.DMA
    scratch = [
        V((2, TOK, NG * PG), BF16),
        V((2, TOK, QHALF), BF16),
        V((2, TOK, QHALF), BF16),
        V((6, TOK, HALF), BF16),
        V((6, TOK, HALF), BF16),
        V((2, 4, HALF), F32),
        V((NZ, 16, 128), BF16),
        V((2, NG, NY, ROWS, HALF), BF16),
        V((2, TOK, 5 * TOK), F32),
        V((PG, PG), BF16),
        V((NG, 2 * TOK, PG), BF16),
        V((NG, PG, 2 * TOK), BF16),
        V((4, 4 * TOK, 5 * TOK), BF16),
        V((4 * TOK, 5 * TOK), BF16),
        V((6, TOK, HALF), F32),
        V((6, TOK, HALF), F32),
        V((2, 4, TOK, DH), BF16),
        V((4, 2, TOK, DH), BF16),
        V((2, 4, TOK, DH), BF16),
        V((8, TOK, DH), BF16),
        V((2, TOK, DH), F32),
        V((2, TOK, DH), F32),
        V((2, TOK, HALF), BF16),
        V((2, TOK, HALF), BF16),
        V((NG, NY, ROWS, HALF), BF16),
        V((NX - 1, NY, ZH, ROWS, HALF), BF16),
        V((NY - 1, ZH, ROWS, HALF), BF16),
        V((NX - 1, ZH, ROWS, HALF), BF16),
        V((ZH, ROWS, HALF), F32),
        V((NZ, 16, 128), BF16),
        V((NZ, 16, 128), BF16),
        V((2, 8, HALF), F32),
        V((2, TOK, QHALF), BF16),
        V((2, TOK, QHALF), BF16),
        V((3, 4, 2 * HALF), F32),
        V((TOK, NG * PG), BF16),
        DMA((11,)),
        DMA((9,)), DMA((9,)),
        DMA((5,)), DMA((6,)),
        DMA((4,)), DMA((4,)),
        DMA((4,)), DMA((4,)),
        DMA((10,)), DMA((10,)),
        DMA((NZ,)), DMA((NZ,)),
        DMA((NX - 1,)), DMA((NX - 1,)),
        DMA((NY * (NX - 1),)), DMA((NY * (NX - 1),)),
        DMA((NY * (NX - 1),)), DMA((NY * (NX - 1),)),
        DMA((NX - 1,)), DMA((NX - 1,)),
        DMA((NZ,)), DMA((NZ,)),
    ]
    hbm = pl.BlockSpec(memory_space=pltpu.HBM)
    anywhere = pl.BlockSpec(memory_space=pl.ANY)
    vmem = pl.BlockSpec(memory_space=pltpu.VMEM)
    outs = (queries, queries, key_rows, hidden, master_value, adam_first, adam_second)
    shapes = tuple(jax.ShapeDtypeStruct(a.shape, a.dtype) for a in outs)
    results = pl.pallas_call(
        kernel,
        out_shape=shapes,
        in_specs=[hbm] * 7,
        out_specs=(anywhere, anywhere, vmem, anywhere, vmem, vmem, vmem),
        scratch_shapes=scratch,
        compiler_params=pltpu.CompilerParams(
            collective_id=0, has_side_effects=True, vmem_limit_bytes=52 * 1024 * 1024
        ),
    )(
        *(
            pltpu.with_memory_space_constraint(a, pltpu.HBM)
            for a in (hidden, queries, key_rows, grad_out, master_value, adam_first, adam_second)
        )
    )
    return pl.pallas_call(
        settle,
        out_shape=shapes,
        in_specs=[anywhere] * 7,
        out_specs=(hbm,) * 7,
        scratch_shapes=[DMA((7,))],
        compiler_params=pltpu.CompilerParams(vmem_limit_bytes=2 * 1024 * 1024),
    )(*results)


def solution(mesh):
    placed = (P("seq", None),) * 7
    return jax.shard_map(
        shards, mesh=mesh, in_specs=placed, out_specs=placed, check_vma=False
    )
```
